512 devices in a mesh: pair: 64 (over y_lo, z, core), mo: 8 (over y_hi, x).
Axes of the slice: x: 4, y: 8 (y_hi: 2, y_lo: 4; y = y_hi * 4 + y_lo), z: 8, core: 2. Of those that a mesh axis runs over, the one named last changes fastest.
Arguments:
- packed: bfloat16 [64, 1024, 2048], P(None, 'pair'), may hold values from -6 to 6
- low_diag: bfloat16 [64, 1024], P(None, 'pair'), may hold values from -12 to 12
- occ_coef: bfloat16 [2048, 256], P('pair', 'mo'), may hold values from -0.125 to 0.125
- vir_coef: bfloat16 [2048, 1792], P('pair', 'mo'), may hold values from -0.125 to 0.125
Outputs:
- half_ints: float32 [64, 256, 1792], P('pair', None, 'mo')
The draws below stay inside these ranges and needn't reach their ends.
All inputs are finite; a program needn't handle non-finite values.
Results may differ from the reference program's by a relative error of at most 0.0029.
Values may be sent and summed in bfloat16 or wider, within the bound.
A program may use at most 64 MiB of HBM per device.

```python
import jax
import jax.numpy as jnp
from jax import lax

N = 2048
NOCC = 256
NVIR = 1792
B = 64


def block_levels(stream_key, dims, cuts, smallest, largest):
    def one(dim, parts):
        steps = jax.random.uniform(jax.random.fold_in(jax.random.fold_in(stream_key, 6), dim), (parts,), jnp.float32, smallest / len(cuts), largest / len(cuts))
        return jnp.repeat(jnp.exp(steps), dims[dim] // parts).reshape((-1,) + (1,) * (len(dims) - dim - 1))

    gain = one(*cuts[0])
    for cut in cuts[1:]:
        gain = gain * one(*cut)
    return gain


def noise(key, extent, scale, reach, shards=(), kind=jnp.bfloat16):
    values = jax.random.normal(key, extent, jnp.float32) * scale
    if len(shards) > 0:
        values = block_levels(key, extent, shards, -0.22, 0.18) * values
    return jnp.clip(values, min=-reach, max=reach).astype(kind)


def setup_inputs(seed: int = 0) -> dict:
    seeds = jax.random.split(jax.random.key(seed), 5)
    packed = noise(seeds[0], (B, N // 2, N), 1.0, 6.0, ((1, 64),))
    low_diag = noise(seeds[1], (B, N // 2), 3.0, 12.0, ((1, 64),))
    occ_coef = noise(seeds[2], (N, NOCC), N ** -0.5, 0.125, ((0, 64), (1, 8)))
    vir_coef = noise(seeds[3], (N, NVIR), N ** -0.5, 0.125, ((0, 64), (1, 8)))
    return {"packed": packed, "low_diag": low_diag, "occ_coef": occ_coef, "vir_coef": vir_coef}


def unpack(packed_rows, diag_part):
    half_basis = N // 2
    row_index = lax.broadcasted_iota(jnp.int32, (half_basis, N), 0)
    col_index = lax.broadcasted_iota(jnp.int32, (half_basis, N), 1)
    hi_pos = half_basis + row_index
    lo_pos = half_basis - 1 - row_index
    hi_rows = jnp.where(col_index < hi_pos, packed_rows, jnp.where(col_index == hi_pos, packed_rows * 0.5, 0))
    flipped = packed_rows[:, ::-1]
    lo_rows = jnp.where(col_index < lo_pos, flipped, jnp.where(col_index == lo_pos, 0.5 * diag_part[:, None], 0))
    return jnp.concatenate([lo_rows[::-1], hi_rows], axis=0).astype(packed_rows.dtype)


def reference(packed, low_diag, occ_coef, vir_coef):
    def single_pair(pair_args):
        packed_rows, diag_part = pair_args
        lower_rows = unpack(packed_rows, diag_part)
        vir_half = jnp.dot(lower_rows, vir_coef, preferred_element_type=jnp.float32).astype(jnp.bfloat16)
        occ_half = jnp.dot(lower_rows, occ_coef, preferred_element_type=jnp.float32).astype(jnp.bfloat16)
        first_term = jnp.dot(occ_coef.T, vir_half, preferred_element_type=jnp.float32)
        second_term = jnp.dot(occ_half.T, vir_coef, preferred_element_type=jnp.float32)
        return first_term + second_term

    return lax.map(single_pair, (packed, low_diag))
```

```python
import functools

import jax
import jax.numpy as jnp
from jax import lax
from jax.experimental import pallas as pl
from jax.experimental.pallas import tpu as pltpu
from jax.sharding import PartitionSpec as P

MESH = pl.DeviceIdType.MESH
BF = jnp.bfloat16
F32 = jnp.float32
YL, YH, NX, NC = 4, 2, 4, 2
YR = YL * YH


def iota(shape, dim):
    return lax.broadcasted_iota(jnp.int32, shape, dim)


def anti_identity(n):
    return (iota((n, n), 0) + iota((n, n), 1) == n - 1).astype(BF)


def kernel(
    pairs, mos, packed, low_diag, occ, vir, out,
    raw, slab, part, p_occ, p_vir, pan, xo, rp_send, rp, acc,
    raw_s, raw_r, slab_s, part_s, part_r, oz_s, oz_r, oy_s, oy_r, oc_s, oc_r,
    vz_s, vz_r, vy_s, vy_r, vc_s, vc_r, rp_s, rp_r, xo_s, xo_r,
):
    nz = pairs // (YL * NC)
    per = pairs // mos
    chunk = 16 * per
    half = pairs * 16
    nocc = occ.shape[1] * mos
    nvir = vir.shape[1]
    p, m = lax.axis_index("pair"), lax.axis_index("mo")
    ylo, z, core = p // (nz * NC), lax.rem(p // NC, nz), lax.rem(p, NC)
    yhi, x = m // NX, lax.rem(m, NX)
    y = yhi * YL + ylo

    def pair_at(y_, z_, c_):
        return (lax.rem(y_, YL) * nz + z_) * NC + c_

    def to(q, k):
        return {"pair": q, "mo": k}

    def along_y(step):
        y_ = lax.rem(y + step + YR, YR)
        return to(pair_at(y_, z, core), (y_ // YL) * NX + x)

    def remote(src, dst, s, r, dev):
        return pltpu.make_async_remote_copy(
            src_ref=src, dst_ref=dst, send_sem=s, recv_sem=r, device_id=dev, device_id_type=MESH
        )

    def take(ref, sem):
        pltpu.make_async_copy(ref, ref, sem).wait()

    barrier = pltpu.get_barrier_semaphore()

    def greet(dev):
        pl.semaphore_signal(barrier, inc=1, device_id=dev, device_id_type=MESH)

    @pl.loop(1, pairs)
    def _(q):
        greet(to(lax.rem(p + q, pairs), m))

    @pl.loop(1, mos)
    def _(q):
        greet(to(p, lax.rem(m + q, mos)))

    for step in (1, -1, 2, -2):
        greet(along_y(step))

    @pl.loop(0, per)
    def _(j):
        @pl.when((m * per + j != p) | (p // per != m))
        def _():
            greet(to(m * per + j, p // per))

    slab_copy = pltpu.make_async_copy(packed.at[pl.ds(m * per, per)], slab, slab_s.at[0])
    slab_copy.start()
    turn = jnp.where(
        p < pairs // 2,
        (iota((32, 32), 0) + iota((32, 32), 1) == 31).astype(F32),
        (iota((32, 32), 0) == iota((32, 32), 1)).astype(F32),
    ).astype(BF)
    spread = (iota((nvir, 256), 0) == iota((nvir, 256), 1)).astype(BF)
    vir_turned = jnp.dot(turn, vir[...], preferred_element_type=F32).astype(BF)
    p_vir[ylo, core, z] = jnp.dot(vir_turned, spread, preferred_element_type=F32).astype(BF)
    spread = (iota((occ.shape[1], 128), 0) == iota((occ.shape[1], 128), 1)).astype(BF)
    part[m] = jnp.dot(occ[...], spread, preferred_element_type=F32).astype(BF)

    pl.semaphore_wait(barrier, pairs - 1 + mos - 1 + 4 + per - (p // per == m).astype(jnp.int32))

    @pl.loop(1, mos)
    def _(q):
        remote(part.at[m], part.at[m], part_s, part_r, to(p, lax.rem(m + q, mos))).start()

    @pl.loop(1, nz)
    def _(q):
        slot = p_vir.at[ylo, core, z]
        remote(slot, slot, vz_s, vz_r, to(pair_at(ylo, lax.rem(z + q, nz), core), m)).start()

    starts = (half - chunk * (m + 1), half + chunk * m)

    def send_raw(side):
        cols = pl.ds(pl.multiple_of(starts[side], 128) if chunk % 128 == 0 else starts[side], chunk)
        rows = pl.ds(pl.multiple_of(p * 16, 16), 16)
        pltpu.make_async_copy(packed.at[p, :, cols], raw.at[side, rows], slab_s.at[1 + side]).start()

        @pl.loop(1, pairs)
        def _(q):
            dest = lax.rem(p + q, pairs)
            remote(
                packed.at[dest, :, cols], raw.at[side, rows], raw_s.at[side], raw_r.at[side], to(dest, m)
            ).start()

    send_raw(0)

    take(part.at[pl.ds(0, mos - 1)], part_r)
    block = jnp.zeros((32, nocc), F32)
    for k in range(mos):
        place = (iota((128, nocc), 0) + k * occ.shape[1] == iota((128, nocc), 1)) & (
            iota((128, nocc), 0) < occ.shape[1]
        )
        block += jnp.dot(part[k], place.astype(BF), preferred_element_type=F32)
    p_occ[ylo, core, z] = jnp.dot(turn, block.astype(BF), preferred_element_type=F32).astype(BF)

    @pl.loop(1, nz)
    def _(q):
        slot = p_occ.at[ylo, core, z]
        remote(slot, slot, oz_s, oz_r, to(pair_at(ylo, lax.rem(z + q, nz), core), m)).start()

    send_raw(1)

    sibling = to(pair_at(ylo, z, 1 - core), m)
    take(p_occ.at[0, 0, pl.ds(0, nz - 1)], oz_r)
    mine = p_occ.at[ylo, core]
    remote(mine, mine, oy_s.at[0], oy_r.at[0], along_y(1)).start()
    remote(mine, mine, oy_s.at[1], oy_r.at[1], along_y(-1)).start()
    remote(mine, mine, oy_s.at[2], oy_r.at[2], along_y(2 - 4 * core)).start()
    remote(mine, mine, oc_s.at[0], oc_r.at[0], sibling).start()

    take(p_vir.at[0, 0, pl.ds(0, nz - 1)], vz_r)

    def pass_vir(s, up, down):
        held = p_vir.at[s, core]

        def go(up_way):
            step = 1 if up_way else -1
            remote(
                held, held, vy_s.at[s, int(up_way)], vy_r.at[s], to(pair_at(ylo + step, z, core), m)
            ).start()

        if up:
            pl.when(ylo < YL - 1)(lambda: go(True))
        if down:
            pl.when(ylo > 0)(lambda: go(False))
        remote(held, held, vc_s.at[s], vc_r.at[s], sibling).start()

    pass_vir(ylo, True, True)

    for k, step in enumerate((-1, 1, 2)):
        theirs = p_occ.at[lax.rem(ylo + step + YL, YL), core]
        take(theirs, oy_r.at[k])
        remote(theirs, theirs, oc_s.at[k + 1], oc_r.at[k + 1], sibling).start()
    for k, step in enumerate((0, -1, 1, 2)):
        take(p_occ.at[lax.rem(ylo + step + YL, YL), 1 - core], oc_r.at[k])

    def blocks_of(k):
        firsts = [pairs // 2 + k * (chunk // 32) + b for b in range(chunk // 32)]
        for q in firsts + [pairs - 1 - q for q in firsts]:
            yield q // (nz * NC), q % NC, q // NC % nz

    for k in range(mos):
        for b, at in enumerate(blocks_of(k)):
            pan[k, b * 32 : (b + 1) * 32] = p_occ[at]

    flip = anti_identity(chunk)
    nothing = jnp.zeros((chunk, chunk), BF)
    slab_copy.wait()
    diag = jnp.sum(
        jnp.where(
            iota((mos, per, 16), 0) == m, low_diag[...].astype(F32).reshape(mos, per, 16), 0.0
        ),
        axis=0,
    )
    diag = jnp.sum(
        jnp.where(
            iota((per, 16, 16), 1) == iota((per, 16, 16), 2),
            jnp.broadcast_to(diag[:, None, :], (per, 16, 16)),
            0.0,
        ),
        axis=2,
        keepdims=True,
    )
    diag = jnp.broadcast_to(diag, (per, 16, chunk)).reshape(chunk, chunk)
    row = p * 16 + lax.rem(iota((chunk, chunk), 0), 16)
    rows_sum = jnp.zeros((2 * chunk, nocc), F32)
    for k in range(mos):
        a = slab[:, :, half + k * chunk : half + (k + 1) * chunk].reshape(chunk, chunk).astype(F32)
        b = slab[:, :, half - (k + 1) * chunk : half - k * chunk].reshape(chunk, chunk)
        b = jnp.dot(b, flip, preferred_element_type=F32).astype(BF)
        col = k * chunk + iota((chunk, chunk), 1)
        a_low = jnp.where(col < row, a, jnp.where(col == row, a * 0.5, 0.0)).astype(BF)
        a_up = jnp.where(col > row, a, jnp.where(col == row, diag, 0.0)).astype(BF)
        left = jnp.concatenate(
            [jnp.concatenate([a_low, b], axis=1), jnp.concatenate([nothing, a_up], axis=1)], axis=0
        )
        rows_sum += jnp.dot(left, pan[k], preferred_element_type=F32)
    rows_sum = rows_sum.astype(BF)
    rp_send[:, 0:16] = rows_sum[:chunk].reshape(per, 16, nocc)
    rp_send[:, 16:32] = rows_sum[chunk:].reshape(per, 16, nocc)

    own_row = lax.rem(p, per)

    @pl.loop(0, per)
    def _(j):
        dst = rp.at[own_row]

        @pl.when((m * per + j == p) & (p // per == m))
        def _():
            pltpu.make_async_copy(rp_send.at[j], dst, rp_r.at[j]).start()

        @pl.when((m * per + j != p) | (p // per != m))
        def _():
            remote(rp_send.at[j], dst, rp_s.at[j], rp_r.at[own_row], to(m * per + j, p // per)).start()

    for d in range(1, YL):
        for sign in (-1, 1):
            s = ylo + sign * d

            @pl.when((s >= 0) & (s < YL))
            def _(s=s, sign=sign):
                take(p_vir.at[s, core], vy_r.at[s])
                pass_vir(s, sign < 0, sign > 0)

    rest = pl.ds(0, (pairs - 1) * 16)
    for side in range(2):
        pltpu.make_async_copy(raw.at[side, pl.ds(0, 16)], raw.at[side, pl.ds(0, 16)], slab_s.at[1 + side]).wait()
        take(raw.at[side, rest], raw_r.at[side])
    total = jnp.zeros((nocc, 2 * chunk), F32)
    for k in range(mos):
        here = slice(k * chunk, (k + 1) * chunk)
        a = raw[1, here].astype(F32)
        b = jnp.dot(raw[0, here], flip, preferred_element_type=F32).astype(BF)
        row = k * chunk + iota((chunk, chunk), 0)
        col = m * chunk + iota((chunk, chunk), 1)
        a_low = jnp.where(col < row, a, jnp.where(col == row, a * 0.5, 0.0)).astype(BF)
        a_up = jnp.where(col > row, a, 0.0).astype(BF)
        right = jnp.concatenate(
            [jnp.concatenate([a_low, b], axis=1), jnp.concatenate([nothing, a_up], axis=1)], axis=0
        )
        total += lax.dot_general(pan[k], right, (((0,), (0,)), ((), ())), preferred_element_type=F32)

    for j in range(per):
        take(rp.at[j], rp_r.at[j])
    hi_rows = rp[:, 0:16].reshape(chunk, nocc).astype(F32)
    lo_rows = rp[:, 16:32].reshape(chunk, nocc).astype(F32)
    total += jnp.concatenate([hi_rows, lo_rows], axis=0).T
    xo[m] = total.astype(BF)

    other = (1 - yhi) * NX

    def round_x(step):
        return to(p, yhi * NX + lax.rem(x + step + NX, NX))

    def slot_of(base, step):
        return xo.at[base + lax.rem(x + step + NX, NX)]

    own, twin = xo.at[m], xo.at[other + x]
    base = yhi * NX
    remote(own, own, xo_s.at[0], xo_r.at[0], to(p, other + x)).start()
    remote(own, own, xo_s.at[1], xo_r.at[1], round_x(1)).start()
    remote(own, own, xo_s.at[2], xo_r.at[2], round_x(-1)).start()

    for s in range(YL):
        take(p_vir.at[s, 1 - core], vc_r.at[s])
    for k in range(mos):
        for b, at in enumerate(blocks_of(k)):
            pan[k, b * 32 : (b + 1) * 32, 0:256] = p_vir[at]

    def add(at):
        acc[...] += jnp.dot(xo[at], pan[at], preferred_element_type=F32)

    acc[...] = jnp.dot(xo[m], pan[m], preferred_element_type=F32)
    take(slot_of(base, -1), xo_r.at[1])
    fwd = slot_of(base, -1)
    remote(fwd, fwd, xo_s.at[3], xo_r.at[3], round_x(1)).start()
    take(twin, xo_r.at[0])
    remote(twin, twin, xo_s.at[4], xo_r.at[4], round_x(1)).start()
    remote(twin, twin, xo_s.at[5], xo_r.at[5], round_x(-1)).start()
    add(base + lax.rem(x + NX - 1, NX))
    add(other + x)
    take(slot_of(base, 1), xo_r.at[2])
    add(base + lax.rem(x + 1, NX))
    take(slot_of(other, 1), xo_r.at[5])
    fwd = slot_of(other, 1)
    remote(fwd, fwd, xo_s.at[6], xo_r.at[6], round_x(-1)).start()
    add(other + lax.rem(x + 1, NX))
    take(slot_of(base, 2), xo_r.at[3])
    add(base + lax.rem(x + 2, NX))
    take(slot_of(other, -1), xo_r.at[4])
    add(other + lax.rem(x + NX - 1, NX))
    take(slot_of(other, 2), xo_r.at[6])
    add(other + lax.rem(x + 2, NX))
    out[0] = acc[:, :nvir]

    take(part.at[pl.ds(0, mos - 1)], part_s)
    take(p_vir.at[0, 0, pl.ds(0, nz - 1)], vz_s)
    take(p_occ.at[0, 0, pl.ds(0, nz - 1)], oz_s)
    for side in range(2):
        take(raw.at[side, rest], raw_s.at[side])
    for k in range(3):
        take(p_occ.at[0, 0], oy_s.at[k])
    for k in range(4):
        take(p_occ.at[0, 0], oc_s.at[k])
        take(p_vir.at[0, 0], vc_s.at[k])

    for s in range(YL):
        @pl.when((s <= ylo) & (ylo < YL - 1))
        def _(s=s):
            take(p_vir.at[0, 0], vy_s.at[s, 1])

        @pl.when((s >= ylo) & (ylo > 0))
        def _(s=s):
            take(p_vir.at[0, 0], vy_s.at[s, 0])

    @pl.loop(0, per)
    def _(j):
        @pl.when((m * per + j != p) | (p // per != m))
        def _():
            take(rp_send.at[j], rp_s.at[j])

    for k in range(7):
        take(xo.at[0], xo_s.at[k])


def shards(pairs, mos, packed, low_diag, occ_coef, vir_coef):
    per = pairs // mos
    chunk = 16 * per
    nz = pairs // (YL * NC)
    nocc = occ_coef.shape[1] * mos
    nvir = vir_coef.shape[1]
    dma = pltpu.SemaphoreType.DMA
    one = dma(())
    vmem = pl.BlockSpec(memory_space=pltpu.VMEM)
    return pl.pallas_call(
        functools.partial(kernel, pairs, mos),
        out_shape=jax.ShapeDtypeStruct((1, nocc, nvir), F32),
        in_specs=[pl.BlockSpec(memory_space=pltpu.HBM), vmem, vmem, vmem],
        out_specs=vmem,
        scratch_shapes=[
            pltpu.VMEM((2, 16 * pairs, chunk), BF),
            pltpu.VMEM((per, 16, packed.shape[2]), BF),
            pltpu.VMEM((mos, 32, 128), BF),
            pltpu.VMEM((YL, NC, nz, 32, nocc), BF),
            pltpu.VMEM((YL, NC, nz, 32, 256), BF),
            pltpu.VMEM((mos, 2 * chunk, 256), BF),
            pltpu.VMEM((mos, nocc, 2 * chunk), BF),
            pltpu.VMEM((per, 32, nocc), BF),
            pltpu.VMEM((per, 32, nocc), BF),
            pltpu.VMEM((nocc, 256), F32),
            dma((2,)), dma((2,)), dma((3,)), one, one, one, one, dma((3,)), dma((3,)),
            dma((4,)), dma((4,)), one, one, dma((YL, 2)), dma((YL,)), dma((YL,)), dma((YL,)),
            dma((per,)), dma((per,)), dma((7,)), dma((7,)),
        ],
        compiler_params=pltpu.CompilerParams(
            collective_id=0, has_side_effects=True, vmem_limit_bytes=40 * 1024 * 1024
        ),
    )(packed, low_diag, occ_coef, vir_coef)


def solution(mesh):
    sizes = dict(mesh.shape)
    placed = (P(None, "pair", None), P(None, "pair"), P("pair", "mo"), P("pair", "mo"))
    return jax.shard_map(
        functools.partial(shards, sizes["pair"], sizes["mo"]),
        mesh=mesh, in_specs=placed, out_specs=P("pair", None, "mo"), check_vma=False,
    )
```

```python
import functools

import jax
import jax.numpy as jnp
from jax import lax
from jax.experimental import pallas as pl
from jax.experimental.pallas import tpu as pltpu
from jax.sharding import PartitionSpec as P

MESH = pl.DeviceIdType.MESH
BF = jnp.bfloat16
F32 = jnp.float32
YL, YH, NX, NC = 4, 2, 4, 2
YR = YL * YH
SCHED = (
    ("vy", 0),
    ("r101", 0),
    ("r001", 2),
    ("vz0", 2),
    ("vz1", 4),
    ("vz2", 5),
    ("vz3", 6),
    ("vz4", 8),
)


def iota(shape, dim):
    return lax.broadcasted_iota(jnp.int32, shape, dim)


def kernel(
    pairs, mos, packed, low_diag_in, occ_in, vir_in, out,
    raw, slab, part, p_occ, p_vir, left, xo, rp_send, rp, acc, occ, vir, low_diag,
    in_s, raw_s, raw_r, raw_l, part_s, part_r, oz_s, oz_r, oy_s, oy_r, oc_s, oc_r,
    vy_s, vy_r, vz_s, vz_r, vc_s, vc_r, rp_s, rp_r, xo_s, xo_r,
):
    nz = pairs // (YL * NC)
    per = pairs // mos
    chunk = 16 * per
    half = pairs * 16
    nocc = occ.shape[1] * mos
    nvir = vir.shape[1]
    p, m = lax.axis_index("pair"), lax.axis_index("mo")

    def place(q):
        return q // (nz * NC), lax.rem(q // NC, nz), lax.rem(q, NC)

    ylo, z, core = place(p)
    yhi, x = m // NX, lax.rem(m, NX)
    y = yhi * YL + ylo

    def pair_at(y_, z_, c_):
        return (lax.rem(y_, YL) * nz + z_) * NC + c_

    def to(q, k):
        return {"pair": q, "mo": k}

    def mo_of(y_):
        return (lax.rem(y_ + YR, YR) // YL) * NX + x

    def along_y(step):
        return to(pair_at(lax.rem(y + step + YR, YR), z, core), mo_of(y + step))

    def shift(q):
        y_, z_, c_ = place(q)
        return lax.rem(z_ + 2 * y_ + c_, mos)

    def block_of(q, k):
        return lax.rem(k + shift(q), mos)

    mine = block_of(p, m)

    def remote(src, dst, s, r, dev):
        return pltpu.make_async_remote_copy(
            src_ref=src, dst_ref=dst, send_sem=s, recv_sem=r, device_id=dev, device_id_type=MESH
        )

    def take(ref, sem):
        pltpu.make_async_copy(ref, ref, sem).wait()

    turnover = lax.rem(p // per - m + mos, mos)

    def target(j):
        y_, c_ = j // NC, lax.rem(j, NC)
        return pair_at(y_, lax.rem(turnover - 2 * y_ - c_ + 2 * mos, mos), c_)

    own_row = lax.rem(p, per)
    keeps = mine == p // per

    def nearest(q, z_even_up):
        d = lax.rem(q // (nz * NC) - ylo + YL, YL)
        far = jnp.where(z_even_up, 2, -2)
        return jnp.where(d == 3, -1, jnp.where(d == 2, far, d))

    slab_copies = [
        pltpu.make_async_copy(packed.at[target(j)], slab.at[j], in_s.at[j]) for j in range(per)
    ]
    small_copies = [
        pltpu.make_async_copy(occ_in, occ, in_s.at[per]),
        pltpu.make_async_copy(vir_in, vir, in_s.at[per + 1]),
        pltpu.make_async_copy(low_diag_in, low_diag, in_s.at[per + 2]),
    ]
    for copy in small_copies + slab_copies:
        copy.start()

    barrier = pltpu.get_barrier_semaphore()

    def greet(dev):
        pl.semaphore_signal(barrier, inc=1, device_id=dev, device_id_type=MESH)

    @pl.loop(1, mos)
    def _(q):
        greet(to(p, lax.rem(m + q, mos)))

    for step in (1, -1, 2, -2):
        greet(along_y(step))

    @pl.loop(1, YL)
    def _(q):
        greet(to(pair_at(ylo + q, z, core), m))

    @pl.loop(1, pairs)
    def _(q):
        source = lax.rem(p + q, pairs)
        even = lax.rem(source // NC, 2) == 0
        greet(to(source, mo_of(y + nearest(source, jnp.logical_not(even)))))

    @pl.loop(0, per)
    def _(j):
        @pl.when(mine * per + j != p)
        def _():
            greet(to(mine * per + j, m))

    for copy in small_copies:
        copy.wait()
    turn = jnp.where(
        p < pairs // 2,
        (iota((32, 32), 0) + iota((32, 32), 1) == 31).astype(F32),
        (iota((32, 32), 0) == iota((32, 32), 1)).astype(F32),
    ).astype(BF)
    spread = (iota((occ.shape[1], 128), 0) == iota((occ.shape[1], 128), 1)).astype(BF)
    part[m] = jnp.dot(occ[...], spread, preferred_element_type=F32).astype(BF)
    spread = (iota((nvir, 256), 0) == iota((nvir, 256), 1)).astype(BF)
    vir_turned = jnp.dot(turn, vir[...], preferred_element_type=F32).astype(BF)
    p_vir[core, z, ylo] = jnp.dot(vir_turned, spread, preferred_element_type=F32).astype(BF)

    pl.semaphore_wait(barrier, pairs - 1 + mos - 1 + 4 + YL - 1 + per - keeps.astype(jnp.int32))

    @pl.loop(1, mos)
    def _(q):
        remote(part.at[m], part.at[m], part_s, part_r, to(p, lax.rem(m + q, mos))).start()

    rows = pl.ds(pl.multiple_of(p * 16, 16), 16)

    def columns(side, b):
        first = half + chunk * b if side else half - chunk * (b + 1)
        return pl.ds(pl.multiple_of(first, 128), chunk)

    for side in range(2):
        pltpu.make_async_copy(
            packed.at[p, :, columns(side, mine)], raw.at[side, rows], raw_l.at[side]
        ).start()

    def send_raw(side, lo, hi):
        even = lax.rem(z, 2) == 0

        @pl.loop(lo, hi)
        def _(q):
            dest = lax.rem(p + q, pairs)
            k = mo_of(y + nearest(dest, even))
            remote(
                packed.at[dest, :, columns(side, block_of(dest, k))], raw.at[side, rows],
                raw_s.at[side], raw_r.at[side], to(dest, k),
            ).start()

    sibling = to(pair_at(ylo, z, 1 - core), m)

    def vir_over_y():
        @pl.loop(1, YL)
        def _(q):
            slot = p_vir.at[core, z, ylo]
            remote(slot, slot, vy_s, vy_r, to(pair_at(ylo + q, z, core), m)).start()

    def vir_on(d, ways):
        for way in range(2) if d else range(1):
            sign = 1 - 2 * way
            group = p_vir.at[core, lax.rem(z - sign * d + nz, nz)]

            def go(way, sign):
                remote(
                    group, group, vz_s.at[d + 1, way], vz_r.at[d + 1, way],
                    to(pair_at(ylo, lax.rem(z + sign + nz, nz), core), m),
                ).start()

            def handle():
                if d:
                    take(group, vz_r.at[d, way])
                if d == 0:
                    go(0, 1)
                    go(1, -1)
                elif d < nz // 2 - 1:
                    go(way, sign)
                elif d == nz // 2 - 1:
                    pl.when(core == way)(lambda: go(way, sign))
                remote(group, group, vc_s, vc_r, sibling).start()

            if d == nz // 2:
                pl.when(core == way)(handle)
            else:
                handle()

    def run(action):
        if action[0] == "r":
            side, part_, parts_ = int(action[1]), int(action[2]), int(action[3])
            send_raw(side, max(1, pairs * part_ // parts_), pairs * (part_ + 1) // parts_)
        elif action == "vy":
            vir_over_y()
        elif action == "vz0":
            take(p_vir.at[0, 0, pl.ds(0, YL - 1)], vy_r)
            vir_on(0, 1)
        else:
            vir_on(int(action[2:]), 2)

    def point(n):
        for action, at in SCHED:
            if at == n:
                run(action)

    point(0)

    take(part.at[pl.ds(0, mos - 1)], part_r)
    block = jnp.zeros((32, nocc), F32)
    for k in range(mos):
        at = (iota((128, nocc), 0) + k * occ.shape[1] == iota((128, nocc), 1)) & (
            iota((128, nocc), 0) < occ.shape[1]
        )
        block += jnp.dot(part[k], at.astype(BF), preferred_element_type=F32)
    p_occ[ylo, core, z] = jnp.dot(turn, block.astype(BF), preferred_element_type=F32).astype(BF)

    order = [1, nz - 1, 2, nz - 2, 3, nz - 3, nz // 2]
    ways_y = (1, -1, 2 - 4 * core)

    def occ_on(q, g):
        got = p_occ.at[ylo, core, lax.rem(z - q + nz, nz)]
        if q:
            take(got, oz_r.at[q])
        for k, step in enumerate(ways_y):
            remote(got, got, oy_s.at[k, g], oy_r.at[k, g], along_y(step)).start()
        remote(got, got, oc_s.at[0, g], oc_r.at[0, g], sibling).start()

    own = p_occ.at[ylo, core, z]
    for q in order:
        remote(own, own, oz_s, oz_r.at[q], to(pair_at(ylo, lax.rem(z + q, nz), core), m)).start()
    occ_on(0, 0)
    point(1)
    for i, q in enumerate(order):
        occ_on(q, int(i >= nz // 2 - 1))
    point(2)

    for copy in slab_copies:
        copy.wait()
    flip = (iota((chunk, chunk), 0) + iota((chunk, chunk), 1) == chunk - 1).astype(BF)
    nothing = jnp.zeros((chunk, chunk), BF)
    diag = jnp.concatenate(
        [
            jnp.sum(
                jnp.where(iota((16, pairs), 1) == target(j), low_diag[...].astype(F32), 0.0),
                axis=1, keepdims=True,
            )
            for j in range(per)
        ],
        axis=0,
    )
    row = p * 16 + lax.rem(iota((chunk, chunk), 0), 16)
    for k in range(mos):
        a = slab[:, :, half + k * chunk : half + (k + 1) * chunk].reshape(chunk, chunk).astype(F32)
        b = slab[:, :, half - (k + 1) * chunk : half - k * chunk].reshape(chunk, chunk)
        b = jnp.dot(b, flip, preferred_element_type=F32).astype(BF)
        col = k * chunk + iota((chunk, chunk), 1)
        a_low = jnp.where(col < row, a, jnp.where(col == row, a * 0.5, 0.0)).astype(BF)
        a_up = jnp.where(col > row, a, jnp.where(col == row, diag, 0.0)).astype(BF)
        left[k] = jnp.concatenate(
            [jnp.concatenate([a_low, b], axis=1), jnp.concatenate([nothing, a_up], axis=1)], axis=0
        )

    far_blocks = [order[i] for i in range(nz // 2 - 1, nz - 1)]
    near_blocks = [0] + [order[i] for i in range(nz // 2 - 1)]
    for g, qs in enumerate((near_blocks, far_blocks)):
        for k, step in enumerate((-1, 1, 2)):
            s_ = lax.rem(ylo + step + YL, YL)
            take(p_occ.at[0, 0, pl.ds(0, len(qs))], oy_r.at[k, g])
            for q in qs:
                theirs = p_occ.at[s_, core, lax.rem(z - q + nz, nz)]
                remote(theirs, theirs, oc_s.at[k + 1, g], oc_r.at[k + 1, g], sibling).start()
    for g, qs in enumerate((near_blocks, far_blocks)):
        for k in range(4):
            take(p_occ.at[0, 0, pl.ds(0, len(qs))], oc_r.at[k, g])
    point(3)

    def blocks_of(k):
        firsts = [pairs // 2 + k * (chunk // 32) + b for b in range(chunk // 32)]
        for q in firsts + [pairs - 1 - q for q in firsts]:
            yield q // (nz * NC), q % NC, q // NC % nz

    def pan(k):
        return jnp.concatenate([p_occ[at] for at in blocks_of(k)], axis=0)

    rows_sum = jnp.zeros((2 * chunk, nocc), F32)
    for k in range(mos):
        rows_sum += jnp.dot(left[k], pan(k), preferred_element_type=F32)
    rows_sum = rows_sum.astype(BF)
    rp_send[:, 0:16] = rows_sum[:chunk].reshape(per, 16, nocc)
    rp_send[:, 16:32] = rows_sum[chunk:].reshape(per, 16, nocc)

    @pl.loop(0, per)
    def _(j):
        dst = rp.at[own_row]

        @pl.when(target(j) == p)
        def _():
            pltpu.make_async_copy(rp_send.at[j], dst, rp_r.at[own_row]).start()

        @pl.when(target(j) != p)
        def _():
            remote(rp_send.at[j], dst, rp_s.at[j], rp_r.at[own_row], to(target(j), m)).start()

    point(4)

    rest = pl.ds(0, (pairs - 1) * 16)

    def wait_raw(side):
        one = raw.at[side, pl.ds(0, 16)]
        pltpu.make_async_copy(one, one, raw_l.at[side]).wait()
        take(raw.at[side, rest], raw_r.at[side])

    def trans_dot(a, b):
        return lax.dot_general(a, b, (((0,), (0,)), ((), ())), preferred_element_type=F32)

    wait_raw(1)
    col = mine * chunk + iota((chunk, chunk), 1)
    hi_sum = jnp.zeros((chunk, nocc), F32)
    for k in range(mos):
        a = raw[1, k * chunk : (k + 1) * chunk].astype(F32)
        row = k * chunk + iota((chunk, chunk), 0)
        a_low = jnp.where(col < row, a, jnp.where(col == row, a * 0.5, 0.0)).astype(BF)
        hi_sum += trans_dot(a_low, pan(k)[:chunk])
    wait_raw(0)
    lo_sum = jnp.zeros((chunk, nocc), F32)
    for k in range(mos):
        here = slice(k * chunk, (k + 1) * chunk)
        a = raw[1, here].astype(F32)
        b = jnp.dot(raw[0, here], flip, preferred_element_type=F32).astype(BF)
        row = k * chunk + iota((chunk, chunk), 0)
        a_up = jnp.where(col > row, a, 0.0).astype(BF)
        lo_sum += trans_dot(jnp.concatenate([b, a_up], axis=0), pan(k))

    other, base = (1 - yhi) * NX, yhi * NX

    def round_x(step):
        return to(p, base + lax.rem(x + step + NX, NX))

    def slot(h, first, step):
        return xo.at[first + lax.rem(x + step + NX, NX), h]

    def send_xo(h, which, ref, dev):
        remote(ref, ref, xo_s.at[h, which], xo_r.at[h, which], dev).start()

    def got_xo(h, which, ref):
        take(ref, xo_r.at[h, which])

    point(5)
    for j in range(per):
        take(rp.at[j], rp_r.at[j])
    for h, column_sum in enumerate((hi_sum, lo_sum)):
        row_sum = rp[:, 16 * h : 16 * h + 16].reshape(chunk, nocc).astype(F32)
        xo[m, h] = (column_sum + row_sum).astype(BF)
        send_xo(h, 0, xo.at[m, h], to(p, other + x))
        send_xo(h, 1, xo.at[m, h], round_x(1))
        send_xo(h, 2, xo.at[m, h], round_x(-1))

    point(6)
    for h in range(2):
        got_xo(h, 1, slot(h, base, -1))
        send_xo(h, 3, slot(h, base, -1), round_x(1))
    point(7)
    for h in range(2):
        twin = xo.at[other + x, h]
        got_xo(h, 0, twin)
        send_xo(h, 4, twin, round_x(1))
        send_xo(h, 5, twin, round_x(-1))
    point(8)

    take(p_vir.at[1 - core], vc_r)
    for k in range(mos):
        left[k] = jnp.concatenate([p_vir[c, z_, y_] for y_, c, z_ in blocks_of(k)], axis=0)

    def add(h, first, step, fresh=False):
        at = first + lax.rem(x + step + NX, NX)
        term = trans_dot(left[block_of(p, at), h * chunk : (h + 1) * chunk], xo[at, h])
        acc[...] = term if fresh else acc[...] + term

    for h in range(2):
        add(h, base, 0, fresh=h == 0)
        add(h, base, -1)
        add(h, other, 0)
    for h in range(2):
        got_xo(h, 2, slot(h, base, 1))
        add(h, base, 1)
        got_xo(h, 5, slot(h, other, 1))
        send_xo(h, 6, slot(h, other, 1), round_x(-1))
        add(h, other, 1)
    for h in range(2):
        got_xo(h, 3, slot(h, base, 2))
        add(h, base, 2)
        got_xo(h, 4, slot(h, other, -1))
        add(h, other, -1)
    for h in range(2):
        got_xo(h, 6, slot(h, other, 2))
        add(h, other, 2)
    out[0] = acc[:nvir]

    take(part.at[pl.ds(0, mos - 1)], part_s)
    take(p_occ.at[0, 0, pl.ds(0, nz - 1)], oz_s)
    for side in range(2):
        take(raw.at[side, rest], raw_s.at[side])
    for g, qs in enumerate((near_blocks, far_blocks)):
        for k in range(3):
            take(p_occ.at[0, 0, pl.ds(0, len(qs))], oy_s.at[k, g])
        for k in range(4):
            take(p_occ.at[0, 0, pl.ds(0, len(qs))], oc_s.at[k, g])
    take(p_vir.at[0, 0, pl.ds(0, YL - 1)], vy_s)
    for d in range(1, nz // 2):
        for way in range(2):
            take(p_vir.at[0, 0], vz_s.at[d, way])
    for way in range(2):
        pl.when(core == way)(lambda way=way: take(p_vir.at[0, 0], vz_s.at[nz // 2, way]))
    take(p_vir.at[core], vc_s)

    @pl.loop(0, per)
    def _(j):
        @pl.when(target(j) != p)
        def _():
            take(rp_send.at[j], rp_s.at[j])

    for h in range(2):
        for k in range(7):
            take(xo.at[0, 0], xo_s.at[h, k])


def shards(pairs, mos, packed, low_diag, occ_coef, vir_coef):
    per = pairs // mos
    chunk = 16 * per
    nz = pairs // (YL * NC)
    nocc = occ_coef.shape[1] * mos
    nvir = vir_coef.shape[1]
    dma = pltpu.SemaphoreType.DMA
    one = dma(())
    hbm = pl.BlockSpec(memory_space=pltpu.HBM)
    return pl.pallas_call(
        functools.partial(kernel, pairs, mos),
        out_shape=jax.ShapeDtypeStruct((1, nvir, nocc), F32),
        in_specs=[hbm] * 4,
        out_specs=pl.BlockSpec(memory_space=pltpu.VMEM),
        scratch_shapes=[
            pltpu.VMEM((2, 16 * pairs, chunk), BF),
            pltpu.VMEM((per, 16, packed.shape[2]), BF),
            pltpu.VMEM((mos, 32, 128), BF),
            pltpu.VMEM((YL, NC, nz, 32, nocc), BF),
            pltpu.VMEM((NC, nz, YL, 32, 256), BF),
            pltpu.VMEM((mos, 2 * chunk, 2 * chunk), BF),
            pltpu.VMEM((mos, 2, chunk, nocc), BF),
            pltpu.VMEM((per, 32, nocc), BF),
            pltpu.VMEM((per, 32, nocc), BF),
            pltpu.VMEM((256, nocc), F32),
            pltpu.VMEM(occ_coef.shape, BF),
            pltpu.VMEM(vir_coef.shape, BF),
            pltpu.VMEM((16, pairs), BF),
            dma((per + 3,)), dma((2,)), dma((2,)), dma((2,)), one, one,
            one, dma((nz,)), dma((3, 2)), dma((3, 2)), dma((4, 2)), dma((4, 2)),
            one, one, dma((nz // 2 + 1, 2)), dma((nz // 2 + 1, 2)), one, one,
            dma((per,)), dma((per,)), dma((2, 7)), dma((2, 7)),
        ],
        compiler_params=pltpu.CompilerParams(
            collective_id=0, has_side_effects=True, vmem_limit_bytes=62 * 1024 * 1024
        ),
    )(packed, low_diag.T, occ_coef, vir_coef).transpose(0, 2, 1)


def solution(mesh):
    sizes = dict(mesh.shape)
    placed = (P(None, "pair", None), P(None, "pair"), P("pair", "mo"), P("pair", "mo"))
    return jax.shard_map(
        functools.partial(shards, sizes["pair"], sizes["mo"]),
        mesh=mesh, in_specs=placed, out_specs=P("pair", None, "mo"), check_vma=False,
    )
```

```python
import functools

import jax
import jax.numpy as jnp
from jax import lax
from jax.experimental import pallas as pl
from jax.experimental.pallas import tpu as pltpu
from jax.sharding import PartitionSpec as P

MESH = pl.DeviceIdType.MESH
BF = jnp.bfloat16
F32 = jnp.float32
YL, YH, NX, NC = 4, 2, 4, 2
YR = YL * YH
SCHED = (
    ("vy", 0),
    ("r101", 0),
    ("r001", 2),
    ("vz0", 4),
    ("vz1", 6),
    ("vz2", 8),
)
NP = 2


def iota(shape, dim):
    return lax.broadcasted_iota(jnp.int32, shape, dim)


def kernel(
    pairs, mos, packed, low_diag_in, occ_in, vir_in, out,
    raw, slab, part, p_occ, p_vir, left, right, xo, rp_send, rp, acc, occ, vir, low_diag,
    in_s, raw_s, raw_r, raw_l, part_s, part_r, oz_s, oz_r, oy_s, oy_r, oc_s, oc_r,
    vy_s, vy_r, vz_s, vz_r, vc_s, vc_r, rp_s, rp_r, xo_s, xo_r,
):
    nz = pairs // (YL * NC)
    per = pairs // mos
    chunk = 16 * per
    half = pairs * 16
    nocc = occ.shape[1] * mos
    nvir = vir.shape[1]
    p, m = lax.axis_index("pair"), lax.axis_index("mo")

    def place(q):
        return q // (nz * NC), lax.rem(q // NC, nz), lax.rem(q, NC)

    ylo, z, core = place(p)
    yhi, x = m // NX, lax.rem(m, NX)
    y = yhi * YL + ylo

    def pair_at(y_, z_, c_):
        return (lax.rem(y_, YL) * nz + z_) * NC + c_

    def to(q, k):
        return {"pair": q, "mo": k}

    def mo_of(y_):
        return (lax.rem(y_ + YR, YR) // YL) * NX + x

    def along_y(step):
        return to(pair_at(lax.rem(y + step + YR, YR), z, core), mo_of(y + step))

    def shift(q):
        y_, z_, c_ = place(q)
        return lax.rem(z_ + 2 * y_ + c_, mos)

    def block_of(q, k):
        return lax.rem(k + shift(q), mos)

    mine = block_of(p, m)

    def remote(src, dst, s, r, dev):
        return pltpu.make_async_remote_copy(
            src_ref=src, dst_ref=dst, send_sem=s, recv_sem=r, device_id=dev, device_id_type=MESH
        )

    def take(ref, sem):
        pltpu.make_async_copy(ref, ref, sem).wait()

    turnover = lax.rem(p // per - m + mos, mos)

    def target(j):
        y_, c_ = j // NC, lax.rem(j, NC)
        return pair_at(y_, lax.rem(turnover - 2 * y_ - c_ + 2 * mos, mos), c_)

    own_row = lax.rem(p, per)
    keeps = mine == p // per

    def nearest(q, z_even_up):
        d = lax.rem(q // (nz * NC) - ylo + YL, YL)
        far = jnp.where(z_even_up, 2, -2)
        return jnp.where(d == 3, -1, jnp.where(d == 2, far, d))

    slab_copies = [
        pltpu.make_async_copy(packed.at[target(j)], slab.at[j], in_s.at[j]) for j in range(per)
    ]
    small_copies = [
        pltpu.make_async_copy(occ_in, occ, in_s.at[per]),
        pltpu.make_async_copy(vir_in, vir, in_s.at[per + 1]),
        pltpu.make_async_copy(low_diag_in, low_diag, in_s.at[per + 2]),
    ]
    for copy in small_copies + slab_copies:
        copy.start()

    barrier = pltpu.get_barrier_semaphore()

    def greet(dev):
        pl.semaphore_signal(barrier, inc=1, device_id=dev, device_id_type=MESH)

    @pl.loop(1, mos)
    def _(q):
        greet(to(p, lax.rem(m + q, mos)))

    for step in (1, -1, 2, -2):
        greet(along_y(step))

    @pl.loop(1, YL)
    def _(q):
        greet(to(pair_at(ylo + q, z, core), m))

    @pl.loop(1, pairs)
    def _(q):
        source = lax.rem(p + q, pairs)
        even = lax.rem(source // NC, 2) == 0
        greet(to(source, mo_of(y + nearest(source, jnp.logical_not(even)))))

    @pl.loop(0, per)
    def _(j):
        @pl.when(mine * per + j != p)
        def _():
            greet(to(mine * per + j, m))

    for copy in small_copies:
        copy.wait()
    turn = jnp.where(
        p < pairs // 2,
        (iota((32, 32), 0) + iota((32, 32), 1) == 31).astype(F32),
        (iota((32, 32), 0) == iota((32, 32), 1)).astype(F32),
    ).astype(BF)
    wide = occ.shape[1]
    part[m] = sum(
        jnp.dot(
            occ[16 * i : 16 * i + 16],
            (iota((wide, 128), 0) + wide * i == iota((wide, 128), 1)).astype(BF),
            preferred_element_type=F32,
        )
        for i in range(2)
    ).astype(BF)
    spread = (iota((nvir, 256), 0) == iota((nvir, 256), 1)).astype(BF)
    vir_turned = jnp.dot(turn, vir[...], preferred_element_type=F32).astype(BF)
    p_vir[core, z, ylo] = jnp.dot(vir_turned, spread, preferred_element_type=F32).astype(BF)

    pl.semaphore_wait(barrier, pairs - 1 + mos - 1 + 4 + YL - 1 + per - keeps.astype(jnp.int32))

    @pl.loop(1, mos)
    def _(q):
        remote(part.at[m], part.at[m], part_s, part_r, to(p, lax.rem(m + q, mos))).start()

    rows = pl.ds(pl.multiple_of(p * 16, 16), 16)

    def columns(side, b):
        first = half + chunk * b if side else half - chunk * (b + 1)
        return pl.ds(pl.multiple_of(first, 128), chunk)

    for side in range(2):
        pltpu.make_async_copy(
            packed.at[p, :, columns(side, mine)], raw.at[side, rows], raw_l.at[side]
        ).start()

    def send_raw(side, lo, hi):
        even = lax.rem(z, 2) == 0

        @pl.loop(lo, hi)
        def _(q):
            dest = lax.rem(p + q * 23, pairs)
            k = mo_of(y + nearest(dest, even))
            remote(
                packed.at[dest, :, columns(side, block_of(dest, k))], raw.at[side, rows],
                raw_s.at[side], raw_r.at[side], to(dest, k),
            ).start()

    sibling = to(pair_at(ylo, z, 1 - core), m)

    def vir_over_y():
        @pl.loop(1, YL)
        def _(q):
            slot = p_vir.at[core, z, ylo]
            remote(slot, slot, vy_s, vy_r, to(pair_at(ylo + q, z, core), m)).start()

    def group(step):
        return p_vir.at[core, lax.rem(z + step + nz, nz)]

    def vir_to(held, i, step):
        dev = to(pair_at(ylo, lax.rem(z + step + nz, nz), core), m)
        remote(held, held, vz_s.at[i], vz_r.at[i], dev).start()

    def vir_to_sibling(held):
        remote(held, held, vc_s, vc_r, sibling).start()

    def vir_near():
        take(p_vir.at[0, 0, pl.ds(0, YL - 1)], vy_r)
        for i, step in enumerate((1, -1, 2, -2)):
            vir_to(group(0), i, step)
        vir_to_sibling(group(0))

    def vir_far():
        for i, step in ((2, 1), (3, -1)):
            held = group(-2 * step)
            take(held, vz_r.at[i])
            vir_to(held, i + 2, step)
            pl.when(core == i - 2)(lambda held=held, step=step: vir_to(held, 6, 2 * step))
            vir_to_sibling(held)
        for i, step in ((0, 1), (1, -1)):
            take(group(-step), vz_r.at[i])
            vir_to_sibling(group(-step))

    def vir_last():
        for i, step in ((4, -3), (5, 3), (6, 4)):
            take(group(step), vz_r.at[i])
            vir_to_sibling(group(step))

    def run(action):
        if action[0] == "r":
            side, part_, parts_ = int(action[1]), int(action[2]), int(action[3])
            send_raw(side, max(1, pairs * part_ // parts_), pairs * (part_ + 1) // parts_)
        elif action == "vy":
            vir_over_y()
        elif action == "vz0":
            vir_near()
        elif action == "vz1":
            vir_far()
        else:
            vir_last()

    def point(n):
        for action, at in SCHED:
            if at == n:
                run(action)

    point(0)

    take(part.at[pl.ds(0, mos - 1)], part_r)
    pair_rows = jnp.zeros((16, 2 * nocc), F32)
    lane, col = iota((128, 2 * nocc), 0), iota((128, 2 * nocc), 1)
    for k in range(mos):
        at = ((lane < wide) & (col == k * wide + lane)) | (
            (lane >= wide) & (lane < 2 * wide) & (col == nocc + (k - 1) * wide + lane)
        )
        pair_rows += jnp.dot(part[k], at.astype(BF), preferred_element_type=F32)
    block = jnp.concatenate([pair_rows[:, :nocc], pair_rows[:, nocc:]], axis=0).astype(BF)
    block = jnp.dot(turn, block, preferred_element_type=F32).astype(BF)
    ncol = nocc // NP
    for h in range(NP):
        p_occ[h, ylo, core, z] = block[:, h * ncol : (h + 1) * ncol]

    order = [1, nz - 1, 2, nz - 2, 3, nz - 3, nz // 2]
    ways_y = (1, -1, 2 - 4 * core)

    def occ_on(h, q):
        got = p_occ.at[h, ylo, core, lax.rem(z - q + nz, nz)]
        if q:
            take(got, oz_r.at[h, q])
        for k, step in enumerate(ways_y):
            remote(got, got, oy_s.at[h, k], oy_r.at[h, k], along_y(step)).start()

    for h in range(NP):
        own = p_occ.at[h, ylo, core, z]
        for q in order:
            remote(
                own, own, oz_s, oz_r.at[h, q], to(pair_at(ylo, lax.rem(z + q, nz), core), m)
            ).start()
        occ_on(h, 0)
    point(1)
    for h in range(NP):
        for q in order:
            occ_on(h, q)
        held = p_occ.at[h, ylo, core]
        remote(held, held, oc_s.at[h, 0], oc_r.at[h, 0], sibling).start()
    point(2)

    for copy in slab_copies:
        copy.wait()
    flip = (iota((chunk, chunk), 0) + iota((chunk, chunk), 1) == chunk - 1).astype(BF)
    nothing = jnp.zeros((chunk, chunk), BF)
    diag = jnp.concatenate(
        [
            jnp.sum(
                jnp.where(iota((16, pairs), 1) == target(j), low_diag[...].astype(F32), 0.0),
                axis=1, keepdims=True,
            )
            for j in range(per)
        ],
        axis=0,
    )
    row = p * 16 + lax.rem(iota((chunk, chunk), 0), 16)
    for k in range(mos):
        a = slab[:, :, half + k * chunk : half + (k + 1) * chunk].reshape(chunk, chunk).astype(F32)
        b = slab[:, :, half - (k + 1) * chunk : half - k * chunk].reshape(chunk, chunk)
        b = jnp.dot(b, flip, preferred_element_type=F32).astype(BF)
        col = k * chunk + iota((chunk, chunk), 1)
        a_low = jnp.where(col < row, a, jnp.where(col == row, a * 0.5, 0.0)).astype(BF)
        a_up = jnp.where(col > row, a, jnp.where(col == row, diag, 0.0)).astype(BF)
        left[k] = jnp.concatenate(
            [jnp.concatenate([a_low, b], axis=1), jnp.concatenate([nothing, a_up], axis=1)], axis=0
        )

    def occ_to_sibling(h):
        for k, step in enumerate((-1, 1, 2)):
            theirs = p_occ.at[h, lax.rem(ylo + step + YL, YL), core]
            take(theirs, oy_r.at[h, k])
            remote(theirs, theirs, oc_s.at[h, k + 1], oc_r.at[h, k + 1], sibling).start()
        for k in range(4):
            take(p_occ.at[0, 0, 0], oc_r.at[h, k])

    def blocks_of(k):
        firsts = [pairs // 2 + k * (chunk // 32) + b for b in range(chunk // 32)]
        for q in firsts + [pairs - 1 - q for q in firsts]:
            yield q // (nz * NC), q % NC, q // NC % nz

    def occ_rows(h, k):
        return jnp.concatenate([p_occ[(h, *at)] for at in blocks_of(k)], axis=0)

    def row_part(h):
        rows_sum = jnp.zeros((2 * chunk, ncol), F32)
        for k in range(mos):
            rows_sum += jnp.dot(left[k], occ_rows(h, k), preferred_element_type=F32)
        rows_sum = rows_sum.astype(BF)
        rp_send[h, :, 0:16] = rows_sum[:chunk].reshape(per, 16, ncol)
        rp_send[h, :, 16:32] = rows_sum[chunk:].reshape(per, 16, ncol)

        @pl.loop(0, per)
        def _(j):
            dst = rp.at[h, own_row]

            @pl.when(target(j) == p)
            def _():
                pltpu.make_async_copy(rp_send.at[h, j], dst, rp_r.at[h, own_row]).start()

            @pl.when(target(j) != p)
            def _():
                remote(
                    rp_send.at[h, j], dst, rp_s.at[h, j], rp_r.at[h, own_row], to(target(j), m)
                ).start()

    for h in range(NP):
        occ_to_sibling(h)
        row_part(h)
        point(3 + h)

    rest = pl.ds(0, (pairs - 1) * 16)
    for side in range(2):
        one = raw.at[side, pl.ds(0, 16)]
        pltpu.make_async_copy(one, one, raw_l.at[side]).wait()
        take(raw.at[side, rest], raw_r.at[side])

    def by_rows(a, b):
        return lax.dot_general(a, b, (((1,), (1,)), ((), ())), preferred_element_type=F32)

    same = (iota((chunk, chunk), 0) == iota((chunk, chunk), 1)).astype(BF)
    here = mine * chunk + iota((chunk, chunk), 0)
    for k in range(mos):
        rows_k = slice(k * chunk, (k + 1) * chunk)
        there = k * chunk + iota((chunk, chunk), 1)
        a = by_rows(same, raw[1, rows_k])
        a_low = jnp.where(here < there, a, jnp.where(here == there, a * 0.5, 0.0)).astype(BF)
        a_up = jnp.where(here > there, a, 0.0).astype(BF)
        b = by_rows(flip, raw[0, rows_k]).astype(BF)
        right[k] = jnp.concatenate(
            [jnp.concatenate([a_low, nothing], axis=1), jnp.concatenate([b, a_up], axis=1)], axis=0
        )
    column_sums = []
    for h in range(NP):
        column_sum = jnp.zeros((2 * chunk, ncol), F32)
        for k in range(mos):
            column_sum += jnp.dot(right[k], occ_rows(h, k), preferred_element_type=F32)
        column_sums.append(column_sum)

    other, base = (1 - yhi) * NX, yhi * NX

    def round_x(step):
        return to(p, base + lax.rem(x + step + NX, NX))

    def slot(h, first, step):
        return xo.at[first + lax.rem(x + step + NX, NX), h]

    def send_xo(h, which, ref, dev):
        remote(ref, ref, xo_s.at[h, which], xo_r.at[h, which], dev).start()

    def got_xo(h, which, ref):
        take(ref, xo_r.at[h, which])

    point(5)
    for h in range(NP):
        for j in range(per):
            take(rp.at[h, j], rp_r.at[h, j])
        row_sum = jnp.concatenate(
            [rp[h, :, 0:16].reshape(chunk, ncol), rp[h, :, 16:32].reshape(chunk, ncol)], axis=0
        )
        xo[m, h] = (column_sums[h] + row_sum.astype(F32)).astype(BF)
        send_xo(h, 0, xo.at[m, h], to(p, other + x))
        send_xo(h, 1, xo.at[m, h], round_x(1))
        send_xo(h, 2, xo.at[m, h], round_x(-1))

    point(6)
    for h in range(NP):
        got_xo(h, 1, slot(h, base, -1))
        send_xo(h, 3, slot(h, base, -1), round_x(1))
    point(7)
    for h in range(NP):
        twin = xo.at[other + x, h]
        got_xo(h, 0, twin)
        send_xo(h, 4, twin, round_x(1))
        send_xo(h, 5, twin, round_x(-1))
        send_xo(h, 6, twin, round_x(2))
    point(8)

    take(p_vir.at[1 - core], vc_r)
    unit = (iota((256, 256), 0) == iota((256, 256), 1)).astype(BF)
    for k in range(mos):
        rows_k = jnp.concatenate([p_vir[c, z_, y_] for y_, c, z_ in blocks_of(k)], axis=0)
        left[k] = by_rows(unit, rows_k).astype(BF)

    def add(h, first, step, fresh=False):
        at = first + lax.rem(x + step + NX, NX)
        term = jnp.dot(left[block_of(p, at)], xo[at, h], preferred_element_type=F32)
        acc[h] = term if fresh else acc[h] + term

    for h in range(NP):
        add(h, base, 0, fresh=True)
        add(h, base, -1)
        add(h, other, 0)
    for h in range(NP):
        got_xo(h, 2, slot(h, base, 1))
        add(h, base, 1)
        got_xo(h, 5, slot(h, other, 1))
        add(h, other, 1)
    for h in range(NP):
        got_xo(h, 3, slot(h, base, 2))
        add(h, base, 2)
        got_xo(h, 4, slot(h, other, -1))
        add(h, other, -1)
    for h in range(NP):
        got_xo(h, 6, slot(h, other, 2))
        add(h, other, 2)
    out[0] = jnp.concatenate([acc[h, :nvir] for h in range(NP)], axis=1)

    take(part.at[pl.ds(0, mos - 1)], part_s)
    for h in range(NP):
        for k in range(3):
            take(p_occ.at[0, 0, 0], oy_s.at[h, k])
        for k in range(4):
            take(p_occ.at[0, 0, 0], oc_s.at[h, k])
    take(p_occ.at[:, 0, 0, pl.ds(0, nz - 1)], oz_s)
    for side in range(2):
        take(raw.at[side, rest], raw_s.at[side])
    take(p_vir.at[0, 0, pl.ds(0, YL - 1)], vy_s)
    for i in range(7):
        take(p_vir.at[0, 0], vz_s.at[i])
    take(p_vir.at[core], vc_s)

    @pl.loop(0, per)
    def _(j):
        @pl.when(target(j) != p)
        def _():
            for h in range(NP):
                take(rp_send.at[h, j], rp_s.at[h, j])

    for h in range(NP):
        for k in range(7):
            take(xo.at[0, 0], xo_s.at[h, k])


def shards(pairs, mos, packed, low_diag, occ_coef, vir_coef):
    per = pairs // mos
    chunk = 16 * per
    nz = pairs // (YL * NC)
    nocc = occ_coef.shape[1] * mos
    nvir = vir_coef.shape[1]
    dma = pltpu.SemaphoreType.DMA
    one = dma(())
    hbm = pl.BlockSpec(memory_space=pltpu.HBM)
    return pl.pallas_call(
        functools.partial(kernel, pairs, mos),
        out_shape=jax.ShapeDtypeStruct((1, nvir, nocc), F32),
        in_specs=[hbm] * 4,
        out_specs=pl.BlockSpec(memory_space=pltpu.VMEM),
        scratch_shapes=[
            pltpu.VMEM((2, 16 * pairs, chunk), BF),
            pltpu.VMEM((per, 16, packed.shape[2]), BF),
            pltpu.VMEM((mos, 16, 128), BF),
            pltpu.VMEM((NP, YL, NC, nz, 32, nocc // NP), BF),
            pltpu.VMEM((NC, nz, YL, 32, 256), BF),
            pltpu.VMEM((mos, 2 * chunk, 2 * chunk), BF),
            pltpu.VMEM((mos, 2 * chunk, 2 * chunk), BF),
            pltpu.VMEM((mos, NP, 2 * chunk, nocc // NP), BF),
            pltpu.VMEM((NP, per, 32, nocc // NP), BF),
            pltpu.VMEM((NP, per, 32, nocc // NP), BF),
            pltpu.VMEM((NP, 256, nocc // NP), F32),
            pltpu.VMEM(occ_coef.shape, BF),
            pltpu.VMEM(vir_coef.shape, BF),
            pltpu.VMEM((16, pairs), BF),
            dma((per + 3,)), dma((2,)), dma((2,)), dma((2,)), one, one,
            one, dma((NP, nz)), dma((NP, 3)), dma((NP, 3)), dma((NP, 4)), dma((NP, 4)),
            one, one, dma((7,)), dma((7,)), one, one,
            dma((NP, per)), dma((NP, per)), dma((NP, 7)), dma((NP, 7)),
        ],
        compiler_params=pltpu.CompilerParams(
            collective_id=0, has_side_effects=True, vmem_limit_bytes=62 * 1024 * 1024
        ),
    )(packed, low_diag.T, occ_coef, vir_coef).transpose(0, 2, 1)


def solution(mesh):
    sizes = dict(mesh.shape)
    placed = (P(None, "pair", None), P(None, "pair"), P("pair", "mo"), P("pair", "mo"))
    return jax.shard_map(
        functools.partial(shards, sizes["pair"], sizes["mo"]),
        mesh=mesh, in_specs=placed, out_specs=P("pair", None, "mo"), check_vma=False,
    )
```

```python
import functools

import jax
import jax.numpy as jnp
from jax import lax
from jax.experimental import pallas as pl
from jax.experimental.pallas import tpu as pltpu
from jax.sharding import PartitionSpec as P

MESH = pl.DeviceIdType.MESH
BF = jnp.bfloat16
F32 = jnp.float32
YL, YH, NX, NC = 4, 2, 4, 2
YR = YL * YH
SCHED = (
    ("vy", 0),
    ("r101", 0),
    ("r001", 2),
    ("vz0", 3),
    ("vz1", 6),
    ("vz2", 8),
)
NP = 2


def iota(shape, dim):
    return lax.broadcasted_iota(jnp.int32, shape, dim)


def kernel(
    pairs, mos, packed, low_diag_in, occ_in, vir_in, out,
    raw, slab, part, p_occ, p_vir, left, right, xo, rp_send, rp, acc, occ, vir, low_diag,
    in_s, raw_s, raw_r, raw_l, part_s, part_r, oz_s, oz_r, oy_s, oy_r, oc_s, oc_r,
    vy_s, vy_r, vz_s, vz_r, vc_s, vc_r, rp_s, rp_r, xo_s, xo_r,
):
    nz = pairs // (YL * NC)
    per = pairs // mos
    chunk = 16 * per
    half = pairs * 16
    nocc = occ.shape[1] * mos
    nvir = vir.shape[1]
    p, m = lax.axis_index("pair"), lax.axis_index("mo")

    def place(q):
        return q // (nz * NC), lax.rem(q // NC, nz), lax.rem(q, NC)

    ylo, z, core = place(p)
    yhi, x = m // NX, lax.rem(m, NX)
    y = yhi * YL + ylo

    def pair_at(y_, z_, c_):
        return (lax.rem(y_, YL) * nz + z_) * NC + c_

    def to(q, k):
        return {"pair": q, "mo": k}

    def mo_of(y_):
        return (lax.rem(y_ + YR, YR) // YL) * NX + x

    def along_y(step):
        return to(pair_at(lax.rem(y + step + YR, YR), z, core), mo_of(y + step))

    def shift(q):
        y_, z_, c_ = place(q)
        return lax.rem(z_ + 2 * y_ + c_, mos)

    def block_of(q, k):
        return lax.rem(k + shift(q), mos)

    mine = block_of(p, m)

    def remote(src, dst, s, r, dev):
        return pltpu.make_async_remote_copy(
            src_ref=src, dst_ref=dst, send_sem=s, recv_sem=r, device_id=dev, device_id_type=MESH
        )

    def take(ref, sem):
        pltpu.make_async_copy(ref, ref, sem).wait()

    turnover = lax.rem(p // per - m + mos, mos)

    def target(j):
        y_, c_ = j // NC, lax.rem(j, NC)
        return pair_at(y_, lax.rem(turnover - 2 * y_ - c_ + 2 * mos, mos), c_)

    own_row = lax.rem(p, per)
    keeps = mine == p // per

    def nearest(q, z_even_up):
        d = lax.rem(q // (nz * NC) - ylo + YL, YL)
        far = jnp.where(z_even_up, 2, -2)
        return jnp.where(d == 3, -1, jnp.where(d == 2, far, d))

    slab_copies = [
        pltpu.make_async_copy(packed.at[target(j)], slab.at[j], in_s.at[j]) for j in range(per)
    ]
    small_copies = [
        pltpu.make_async_copy(occ_in, occ, in_s.at[per]),
        pltpu.make_async_copy(vir_in, vir, in_s.at[per + 1]),
        pltpu.make_async_copy(low_diag_in, low_diag, in_s.at[per + 2]),
    ]
    for copy in small_copies + slab_copies:
        copy.start()

    barrier = pltpu.get_barrier_semaphore()

    def greet(dev):
        pl.semaphore_signal(barrier, inc=1, device_id=dev, device_id_type=MESH)

    @pl.loop(1, mos)
    def _(q):
        greet(to(p, lax.rem(m + q, mos)))

    for step in (1, -1, 2, -2):
        greet(along_y(step))

    @pl.loop(1, YL)
    def _(q):
        greet(to(pair_at(ylo + q, z, core), m))

    @pl.loop(1, pairs)
    def _(q):
        source = lax.rem(p + q, pairs)
        even = lax.rem(source // NC, 2) == 0
        greet(to(source, mo_of(y + nearest(source, jnp.logical_not(even)))))

    @pl.loop(0, per)
    def _(j):
        @pl.when(mine * per + j != p)
        def _():
            greet(to(mine * per + j, m))

    for copy in small_copies:
        copy.wait()
    turn = jnp.where(
        p < pairs // 2,
        (iota((32, 32), 0) + iota((32, 32), 1) == 31).astype(F32),
        (iota((32, 32), 0) == iota((32, 32), 1)).astype(F32),
    ).astype(BF)
    wide = occ.shape[1]
    part[m] = sum(
        jnp.dot(
            occ[16 * i : 16 * i + 16],
            (iota((wide, 128), 0) + wide * i == iota((wide, 128), 1)).astype(BF),
            preferred_element_type=F32,
        )
        for i in range(2)
    ).astype(BF)
    spread = (iota((nvir, 256), 0) == iota((nvir, 256), 1)).astype(BF)
    vir_turned = jnp.dot(turn, vir[...], preferred_element_type=F32).astype(BF)
    p_vir[core, z, ylo] = jnp.dot(vir_turned, spread, preferred_element_type=F32).astype(BF)

    pl.semaphore_wait(barrier, pairs - 1 + mos - 1 + 4 + YL - 1 + per - keeps.astype(jnp.int32))

    @pl.loop(1, mos)
    def _(q):
        remote(part.at[m], part.at[m], part_s, part_r, to(p, lax.rem(m + q, mos))).start()

    rows = pl.ds(pl.multiple_of(p * 16, 16), 16)

    def columns(side, b):
        first = half + chunk * b if side else half - chunk * (b + 1)
        return pl.ds(pl.multiple_of(first, 128), chunk)

    for side in range(2):
        pltpu.make_async_copy(
            packed.at[p, :, columns(side, mine)], raw.at[side, rows], raw_l.at[side]
        ).start()

    def send_raw(side, lo, hi):
        even = lax.rem(z, 2) == 0

        @pl.loop(lo, hi)
        def _(q):
            dest = lax.rem(p + q * 23, pairs)
            k = mo_of(y + nearest(dest, even))
            remote(
                packed.at[dest, :, columns(side, block_of(dest, k))], raw.at[side, rows],
                raw_s.at[side], raw_r.at[side], to(dest, k),
            ).start()

    sibling = to(pair_at(ylo, z, 1 - core), m)

    def vir_over_y():
        @pl.loop(1, YL)
        def _(q):
            slot = p_vir.at[core, z, ylo]
            remote(slot, slot, vy_s, vy_r, to(pair_at(ylo + q, z, core), m)).start()

    def group(step):
        return p_vir.at[core, lax.rem(z + step + nz, nz)]

    def vir_to(held, i, step):
        dev = to(pair_at(ylo, lax.rem(z + step + nz, nz), core), m)
        remote(held, held, vz_s.at[i], vz_r.at[i], dev).start()

    def vir_to_sibling(held):
        remote(held, held, vc_s, vc_r, sibling).start()

    def vir_near():
        take(p_vir.at[0, 0, pl.ds(0, YL - 1)], vy_r)
        for i, step in enumerate((1, -1, 2, -2)):
            vir_to(group(0), i, step)
        vir_to_sibling(group(0))

    def vir_far():
        for i, step in ((2, 1), (3, -1)):
            held = group(-2 * step)
            take(held, vz_r.at[i])
            vir_to(held, i + 2, step)
            pl.when(core == i - 2)(lambda held=held, step=step: vir_to(held, 6, 2 * step))
            vir_to_sibling(held)
        for i, step in ((0, 1), (1, -1)):
            take(group(-step), vz_r.at[i])
            vir_to_sibling(group(-step))

    def vir_last():
        for i, step in ((4, -3), (5, 3), (6, 4)):
            take(group(step), vz_r.at[i])
            vir_to_sibling(group(step))

    def run(action):
        if action[0] == "r":
            side, part_, parts_ = int(action[1]), int(action[2]), int(action[3])
            send_raw(side, max(1, pairs * part_ // parts_), pairs * (part_ + 1) // parts_)
        elif action == "vy":
            vir_over_y()
        elif action == "vz0":
            vir_near()
        elif action == "vz1":
            vir_far()
        else:
            vir_last()

    def point(n):
        for action, at in SCHED:
            if at == n:
                run(action)

    point(0)

    take(part.at[pl.ds(0, mos - 1)], part_r)
    pair_rows = jnp.zeros((16, 2 * nocc), F32)
    lane, col = iota((128, 2 * nocc), 0), iota((128, 2 * nocc), 1)
    for k in range(mos):
        at = ((lane < wide) & (col == k * wide + lane)) | (
            (lane >= wide) & (lane < 2 * wide) & (col == nocc + (k - 1) * wide + lane)
        )
        pair_rows += jnp.dot(part[k], at.astype(BF), preferred_element_type=F32)
    block = jnp.concatenate([pair_rows[:, :nocc], pair_rows[:, nocc:]], axis=0).astype(BF)
    block = jnp.dot(turn, block, preferred_element_type=F32).astype(BF)
    ncol = nocc // NP
    for h in range(NP):
        p_occ[h, ylo, core, z] = block[:, h * ncol : (h + 1) * ncol]

    order = [1, nz - 1, 2, nz - 2, 3, nz - 3, nz // 2]
    ways_y = (1, -1, 2 - 4 * core)

    def occ_on(h, q):
        got = p_occ.at[h, ylo, core, lax.rem(z - q + nz, nz)]
        if q:
            take(got, oz_r.at[h, q])
        for k, step in enumerate(ways_y):
            remote(got, got, oy_s.at[h, k], oy_r.at[h, k], along_y(step)).start()

    for h in range(NP):
        own = p_occ.at[h, ylo, core, z]
        for q in order:
            remote(
                own, own, oz_s, oz_r.at[h, q], to(pair_at(ylo, lax.rem(z + q, nz), core), m)
            ).start()
        occ_on(h, 0)
    point(1)
    for h in range(NP):
        for q in order:
            occ_on(h, q)
        held = p_occ.at[h, ylo, core]
        remote(held, held, oc_s.at[h, 0], oc_r.at[h, 0], sibling).start()
    point(2)

    for copy in slab_copies:
        copy.wait()
    flip = (iota((chunk, chunk), 0) + iota((chunk, chunk), 1) == chunk - 1).astype(BF)
    nothing = jnp.zeros((chunk, chunk), BF)
    diag = jnp.concatenate(
        [
            jnp.sum(
                jnp.where(iota((16, pairs), 1) == target(j), low_diag[...].astype(F32), 0.0),
                axis=1, keepdims=True,
            )
            for j in range(per)
        ],
        axis=0,
    )
    row = p * 16 + lax.rem(iota((chunk, chunk), 0), 16)
    for k in range(mos):
        a = slab[:, :, half + k * chunk : half + (k + 1) * chunk].reshape(chunk, chunk).astype(F32)
        b = slab[:, :, half - (k + 1) * chunk : half - k * chunk].reshape(chunk, chunk)
        b = jnp.dot(b, flip, preferred_element_type=F32).astype(BF)
        col = k * chunk + iota((chunk, chunk), 1)
        a_low = jnp.where(col < row, a, jnp.where(col == row, a * 0.5, 0.0)).astype(BF)
        a_up = jnp.where(col > row, a, jnp.where(col == row, diag, 0.0)).astype(BF)
        left[k] = jnp.concatenate(
            [jnp.concatenate([a_low, b], axis=1), jnp.concatenate([nothing, a_up], axis=1)], axis=0
        )

    rest = pl.ds(0, (pairs - 1) * 16)

    def wait_raw(side):
        one = raw.at[side, pl.ds(0, 16)]
        pltpu.make_async_copy(one, one, raw_l.at[side]).wait()
        take(raw.at[side, rest], raw_r.at[side])

    def by_rows(a, b):
        return lax.dot_general(a, b, (((1,), (1,)), ((), ())), preferred_element_type=F32)

    def prepare_columns():
        same = (iota((chunk, chunk), 0) == iota((chunk, chunk), 1)).astype(BF)
        here = mine * chunk + iota((chunk, chunk), 0)
        wait_raw(1)
        for k in range(mos):
            there = k * chunk + iota((chunk, chunk), 1)
            a = by_rows(same, raw[1, k * chunk : (k + 1) * chunk])
            a_low = jnp.where(here < there, a, jnp.where(here == there, a * 0.5, 0.0))
            right[k, :chunk, :chunk] = a_low.astype(BF)
            right[k, :chunk, chunk:] = nothing
            right[k, chunk:, chunk:] = jnp.where(here > there, a, 0.0).astype(BF)

    prepare_columns()

    def occ_to_sibling(h):
        for k, step in enumerate((-1, 1, 2)):
            theirs = p_occ.at[h, lax.rem(ylo + step + YL, YL), core]
            take(theirs, oy_r.at[h, k])
            remote(theirs, theirs, oc_s.at[h, k + 1], oc_r.at[h, k + 1], sibling).start()
        for k in range(4):
            take(p_occ.at[0, 0, 0], oc_r.at[h, k])

    def blocks_of(k):
        firsts = [pairs // 2 + k * (chunk // 32) + b for b in range(chunk // 32)]
        for q in firsts + [pairs - 1 - q for q in firsts]:
            yield q // (nz * NC), q % NC, q // NC % nz

    def occ_rows(h, k):
        return jnp.concatenate([p_occ[(h, *at)] for at in blocks_of(k)], axis=0)

    def row_part(h):
        rows_sum = jnp.zeros((2 * chunk, ncol), F32)
        for k in range(mos):
            rows_sum += jnp.dot(left[k], occ_rows(h, k), preferred_element_type=F32)
        rows_sum = rows_sum.astype(BF)
        rp_send[h, :, 0:16] = rows_sum[:chunk].reshape(per, 16, ncol)
        rp_send[h, :, 16:32] = rows_sum[chunk:].reshape(per, 16, ncol)

        @pl.loop(0, per)
        def _(j):
            dst = rp.at[h, own_row]

            @pl.when(target(j) == p)
            def _():
                pltpu.make_async_copy(rp_send.at[h, j], dst, rp_r.at[h, own_row]).start()

            @pl.when(target(j) != p)
            def _():
                remote(
                    rp_send.at[h, j], dst, rp_s.at[h, j], rp_r.at[h, own_row], to(target(j), m)
                ).start()

    for h in range(NP):
        occ_to_sibling(h)
        row_part(h)
        point(3 + h)

    wait_raw(0)
    for k in range(mos):
        b = by_rows(flip, raw[0, k * chunk : (k + 1) * chunk]).astype(BF)
        right[k, chunk:, :chunk] = b
    column_sums = []
    for h in range(NP):
        column_sum = jnp.zeros((2 * chunk, ncol), F32)
        for k in range(mos):
            column_sum += jnp.dot(right[k], occ_rows(h, k), preferred_element_type=F32)
        column_sums.append(column_sum)

    other, base = (1 - yhi) * NX, yhi * NX

    def round_x(step):
        return to(p, base + lax.rem(x + step + NX, NX))

    def slot(h, first, step):
        return xo.at[first + lax.rem(x + step + NX, NX), h]

    def send_xo(h, which, ref, dev):
        remote(ref, ref, xo_s.at[h, which], xo_r.at[h, which], dev).start()

    def got_xo(h, which, ref):
        take(ref, xo_r.at[h, which])

    point(5)
    for h in range(NP):
        for j in range(per):
            take(rp.at[h, j], rp_r.at[h, j])
        row_sum = jnp.concatenate(
            [rp[h, :, 0:16].reshape(chunk, ncol), rp[h, :, 16:32].reshape(chunk, ncol)], axis=0
        )
        xo[m, h] = (column_sums[h] + row_sum.astype(F32)).astype(BF)
        send_xo(h, 0, xo.at[m, h], to(p, other + x))
        send_xo(h, 1, xo.at[m, h], round_x(1))
        send_xo(h, 2, xo.at[m, h], round_x(-1))
        send_xo(h, 3, xo.at[m, h], round_x(2))

    point(6)
    for h in range(NP):
        twin = xo.at[other + x, h]
        got_xo(h, 0, twin)
        send_xo(h, 4, twin, round_x(1))
        send_xo(h, 5, twin, round_x(-1))
        send_xo(h, 6, twin, round_x(2))
        if h == 0:
            point(7)
    point(8)

    take(p_vir.at[1 - core], vc_r)
    unit = (iota((256, 256), 0) == iota((256, 256), 1)).astype(BF)
    for k in range(mos):
        rows_k = jnp.concatenate([p_vir[c, z_, y_] for y_, c, z_ in blocks_of(k)], axis=0)
        left[k] = by_rows(unit, rows_k).astype(BF)

    def add(h, first, step, fresh=False):
        at = first + lax.rem(x + step + NX, NX)
        term = jnp.dot(left[block_of(p, at)], xo[at, h], preferred_element_type=F32)
        acc[h] = term if fresh else acc[h] + term

    for h in range(NP):
        add(h, base, 0, fresh=True)
        got_xo(h, 1, slot(h, base, -1))
        add(h, base, -1)
        add(h, other, 0)
    for h in range(NP):
        got_xo(h, 2, slot(h, base, 1))
        add(h, base, 1)
        got_xo(h, 5, slot(h, other, 1))
        add(h, other, 1)
    for h in range(NP):
        got_xo(h, 3, slot(h, base, 2))
        add(h, base, 2)
        got_xo(h, 4, slot(h, other, -1))
        add(h, other, -1)
    for h in range(NP):
        got_xo(h, 6, slot(h, other, 2))
        add(h, other, 2)
    out[0] = jnp.concatenate([acc[h, :nvir] for h in range(NP)], axis=1)

    take(part.at[pl.ds(0, mos - 1)], part_s)
    for h in range(NP):
        for k in range(3):
            take(p_occ.at[0, 0, 0], oy_s.at[h, k])
        for k in range(4):
            take(p_occ.at[0, 0, 0], oc_s.at[h, k])
    take(p_occ.at[:, 0, 0, pl.ds(0, nz - 1)], oz_s)
    for side in range(2):
        take(raw.at[side, rest], raw_s.at[side])
    take(p_vir.at[0, 0, pl.ds(0, YL - 1)], vy_s)
    for i in range(7):
        take(p_vir.at[0, 0], vz_s.at[i])
    take(p_vir.at[core], vc_s)

    @pl.loop(0, per)
    def _(j):
        @pl.when(target(j) != p)
        def _():
            for h in range(NP):
                take(rp_send.at[h, j], rp_s.at[h, j])

    for h in range(NP):
        for k in range(7):
            take(xo.at[0, 0], xo_s.at[h, k])


def shards(pairs, mos, packed, low_diag, occ_coef, vir_coef):
    per = pairs // mos
    chunk = 16 * per
    nz = pairs // (YL * NC)
    nocc = occ_coef.shape[1] * mos
    nvir = vir_coef.shape[1]
    dma = pltpu.SemaphoreType.DMA
    one = dma(())
    hbm = pl.BlockSpec(memory_space=pltpu.HBM)
    return pl.pallas_call(
        functools.partial(kernel, pairs, mos),
        out_shape=jax.ShapeDtypeStruct((1, nvir, nocc), F32),
        in_specs=[hbm] * 4,
        out_specs=pl.BlockSpec(memory_space=pltpu.VMEM),
        scratch_shapes=[
            pltpu.VMEM((2, 16 * pairs, chunk), BF),
            pltpu.VMEM((per, 16, packed.shape[2]), BF),
            pltpu.VMEM((mos, 16, 128), BF),
            pltpu.VMEM((NP, YL, NC, nz, 32, nocc // NP), BF),
            pltpu.VMEM((NC, nz, YL, 32, 256), BF),
            pltpu.VMEM((mos, 2 * chunk, 2 * chunk), BF),
            pltpu.VMEM((mos, 2 * chunk, 2 * chunk), BF),
            pltpu.VMEM((mos, NP, 2 * chunk, nocc // NP), BF),
            pltpu.VMEM((NP, per, 32, nocc // NP), BF),
            pltpu.VMEM((NP, per, 32, nocc // NP), BF),
            pltpu.VMEM((NP, 256, nocc // NP), F32),
            pltpu.VMEM(occ_coef.shape, BF),
            pltpu.VMEM(vir_coef.shape, BF),
            pltpu.VMEM((16, pairs), BF),
            dma((per + 3,)), dma((2,)), dma((2,)), dma((2,)), one, one,
            one, dma((NP, nz)), dma((NP, 3)), dma((NP, 3)), dma((NP, 4)), dma((NP, 4)),
            one, one, dma((7,)), dma((7,)), one, one,
            dma((NP, per)), dma((NP, per)), dma((NP, 7)), dma((NP, 7)),
        ],
        compiler_params=pltpu.CompilerParams(
            collective_id=0, has_side_effects=True, vmem_limit_bytes=62 * 1024 * 1024
        ),
    )(packed, low_diag.T, occ_coef, vir_coef).transpose(0, 2, 1)


def solution(mesh):
    sizes = dict(mesh.shape)
    placed = (P(None, "pair", None), P(None, "pair"), P("pair", "mo"), P("pair", "mo"))
    return jax.shard_map(
        functools.partial(shards, sizes["pair"], sizes["mo"]),
        mesh=mesh, in_specs=placed, out_specs=P("pair", None, "mo"), check_vma=False,
    )
```

```python
import functools

import jax
import jax.numpy as jnp
from jax import lax
from jax.experimental import pallas as pl
from jax.experimental.pallas import tpu as pltpu
from jax.sharding import PartitionSpec as P

MESH = pl.DeviceIdType.MESH
BF = jnp.bfloat16
F32 = jnp.float32
YL, YH, NX, NC = 4, 2, 4, 2
YR = YL * YH
SCHED = (
    ("vy", 0),
    ("r101", 0),
    ("r001", 2),
    ("vz0", 3),
    ("vz1", 6),
    ("vz2", 8),
)
NP = 2


def iota(shape, dim):
    return lax.broadcasted_iota(jnp.int32, shape, dim)


def kernel(
    pairs, mos, packed, low_diag_in, occ_in, vir_in, out,
    raw, slab, part, p_occ, p_vir, left, right, xo, rp_send, rp, acc, occ, vir, low_diag,
    in_s, raw_s, raw_r, raw_l, part_s, part_r, oz_s, oz_r, oy_s, oy_r, oc_s, oc_r,
    vy_s, vy_r, vz_s, vz_r, vc_s, vc_r, rp_s, rp_r, xo_s, xo_r,
):
    nz = pairs // (YL * NC)
    per = pairs // mos
    chunk = 16 * per
    half = pairs * 16
    nocc = occ.shape[1] * mos
    nvir = vir.shape[1]
    p, m = lax.axis_index("pair"), lax.axis_index("mo")

    def place(q):
        return q // (nz * NC), lax.rem(q // NC, nz), lax.rem(q, NC)

    ylo, z, core = place(p)
    yhi, x = m // NX, lax.rem(m, NX)
    y = yhi * YL + ylo

    def pair_at(y_, z_, c_):
        return (lax.rem(y_, YL) * nz + z_) * NC + c_

    def to(q, k):
        return {"pair": q, "mo": k}

    def mo_of(y_):
        return (lax.rem(y_ + YR, YR) // YL) * NX + x

    def along_y(step):
        return to(pair_at(lax.rem(y + step + YR, YR), z, core), mo_of(y + step))

    def shift(q):
        y_, z_, c_ = place(q)
        return lax.rem(z_ + 2 * y_ + c_, mos)

    def block_of(q, k):
        return lax.rem(k + shift(q), mos)

    mine = block_of(p, m)

    def remote(src, dst, s, r, dev):
        return pltpu.make_async_remote_copy(
            src_ref=src, dst_ref=dst, send_sem=s, recv_sem=r, device_id=dev, device_id_type=MESH
        )

    def take(ref, sem):
        pltpu.make_async_copy(ref, ref, sem).wait()

    turnover = lax.rem(p // per - m + mos, mos)

    def target(j):
        y_, c_ = j // NC, lax.rem(j, NC)
        return pair_at(y_, lax.rem(turnover - 2 * y_ - c_ + 2 * mos, mos), c_)

    own_row = lax.rem(p, per)
    keeps = mine == p // per

    def nearest(q, z_even_up):
        d = lax.rem(q // (nz * NC) - ylo + YL, YL)
        far = jnp.where(z_even_up, 2, -2)
        return jnp.where(d == 3, -1, jnp.where(d == 2, far, d))

    slab_copies = [
        pltpu.make_async_copy(packed.at[target(j)], slab.at[j], in_s.at[j]) for j in range(per)
    ]
    small_copies = [
        pltpu.make_async_copy(occ_in, occ, in_s.at[per]),
        pltpu.make_async_copy(vir_in, vir, in_s.at[per + 1]),
        pltpu.make_async_copy(low_diag_in, low_diag, in_s.at[per + 2]),
    ]
    for copy in small_copies + slab_copies:
        copy.start()

    barrier = pltpu.get_barrier_semaphore()

    def greet(dev):
        pl.semaphore_signal(barrier, inc=1, device_id=dev, device_id_type=MESH)

    @pl.loop(1, mos)
    def _(q):
        greet(to(p, lax.rem(m + q, mos)))

    for step in (1, -1, 2, -2):
        greet(along_y(step))

    @pl.loop(1, YL)
    def _(q):
        greet(to(pair_at(ylo + q, z, core), m))

    @pl.loop(1, pairs)
    def _(q):
        source = lax.rem(p + q, pairs)
        even = lax.rem(source // NC, 2) == 0
        greet(to(source, mo_of(y + nearest(source, jnp.logical_not(even)))))

    @pl.loop(0, per)
    def _(j):
        @pl.when(mine * per + j != p)
        def _():
            greet(to(mine * per + j, m))

    for copy in small_copies:
        copy.wait()
    turn = jnp.where(
        p < pairs // 2,
        (iota((32, 32), 0) + iota((32, 32), 1) == 31).astype(F32),
        (iota((32, 32), 0) == iota((32, 32), 1)).astype(F32),
    ).astype(BF)
    wide = occ.shape[1]
    part[m] = sum(
        jnp.dot(
            occ[16 * i : 16 * i + 16],
            (iota((wide, 128), 0) + wide * i == iota((wide, 128), 1)).astype(BF),
            preferred_element_type=F32,
        )
        for i in range(2)
    ).astype(BF)
    spread = (iota((nvir, 256), 0) == iota((nvir, 256), 1)).astype(BF)
    vir_turned = jnp.dot(turn, vir[...], preferred_element_type=F32).astype(BF)
    p_vir[core, z, ylo] = jnp.dot(vir_turned, spread, preferred_element_type=F32).astype(BF)

    pl.semaphore_wait(barrier, pairs - 1 + mos - 1 + 4 + YL - 1 + per - keeps.astype(jnp.int32))

    @pl.loop(1, mos)
    def _(q):
        remote(part.at[m], part.at[m], part_s, part_r, to(p, lax.rem(m + q, mos))).start()

    rows = pl.ds(pl.multiple_of(p * 16, 16), 16)

    def columns(side, b):
        first = half + chunk * b if side else half - chunk * (b + 1)
        return pl.ds(pl.multiple_of(first, 128), chunk)

    for side in range(2):
        pltpu.make_async_copy(
            packed.at[p, :, columns(side, mine)], raw.at[side, rows], raw_l.at[side]
        ).start()

    def send_raw(side, lo, hi):
        even = lax.rem(z, 2) == 0

        @pl.loop(lo, hi)
        def _(q):
            dest = lax.rem(p + q * 23, pairs)
            k = mo_of(y + nearest(dest, even))
            remote(
                packed.at[dest, :, columns(side, block_of(dest, k))], raw.at[side, rows],
                raw_s.at[side], raw_r.at[side], to(dest, k),
            ).start()

    sibling = to(pair_at(ylo, z, 1 - core), m)

    def vir_over_y():
        @pl.loop(1, YL)
        def _(q):
            slot = p_vir.at[core, z, ylo]
            remote(slot, slot, vy_s, vy_r, to(pair_at(ylo + q, z, core), m)).start()

    def group(step):
        return p_vir.at[core, lax.rem(z + step + nz, nz)]

    def vir_to(held, i, step):
        dev = to(pair_at(ylo, lax.rem(z + step + nz, nz), core), m)
        remote(held, held, vz_s.at[i], vz_r.at[i], dev).start()

    def vir_to_sibling(held):
        remote(held, held, vc_s, vc_r, sibling).start()

    def vir_near():
        take(p_vir.at[0, 0, pl.ds(0, YL - 1)], vy_r)
        for i, step in enumerate((1, -1, 2, -2)):
            vir_to(group(0), i, step)
        vir_to_sibling(group(0))

    def vir_far():
        for i, step in ((2, 1), (3, -1)):
            held = group(-2 * step)
            take(held, vz_r.at[i])
            vir_to(held, i + 2, step)
            pl.when(core == i - 2)(lambda held=held, step=step: vir_to(held, 6, 2 * step))
            vir_to_sibling(held)
        for i, step in ((0, 1), (1, -1)):
            take(group(-step), vz_r.at[i])
            vir_to_sibling(group(-step))

    def vir_last():
        for i, step in ((4, -3), (5, 3), (6, 4)):
            take(group(step), vz_r.at[i])
            vir_to_sibling(group(step))

    def run(action):
        if action[0] == "r":
            side, part_, parts_ = int(action[1]), int(action[2]), int(action[3])
            send_raw(side, max(1, pairs * part_ // parts_), pairs * (part_ + 1) // parts_)
        elif action == "vy":
            vir_over_y()
        elif action == "vz0":
            vir_near()
        elif action == "vz1":
            vir_far()
        else:
            vir_last()

    def point(n):
        for action, at in SCHED:
            if at == n:
                run(action)

    point(0)

    take(part.at[pl.ds(0, mos - 1)], part_r)
    pair_rows = jnp.zeros((16, 2 * nocc), F32)
    lane, col = iota((128, 2 * nocc), 0), iota((128, 2 * nocc), 1)
    for k in range(mos):
        at = ((lane < wide) & (col == k * wide + lane)) | (
            (lane >= wide) & (lane < 2 * wide) & (col == nocc + (k - 1) * wide + lane)
        )
        pair_rows += jnp.dot(part[k], at.astype(BF), preferred_element_type=F32)
    block = jnp.concatenate([pair_rows[:, :nocc], pair_rows[:, nocc:]], axis=0).astype(BF)
    block = jnp.dot(turn, block, preferred_element_type=F32).astype(BF)
    ncol = nocc // NP
    for h in range(NP):
        p_occ[h, ylo, core, z] = block[:, h * ncol : (h + 1) * ncol]

    order = [1, nz - 1, 2, nz - 2, 3, nz - 3, nz // 2]
    ways_y = (1, -1, 2 - 4 * core)

    def occ_on(h, q):
        got = p_occ.at[h, ylo, core, lax.rem(z - q + nz, nz)]
        if q:
            take(got, oz_r.at[h, q])
        for k, step in enumerate(ways_y):
            remote(got, got, oy_s.at[h, k], oy_r.at[h, k], along_y(step)).start()

    for h in range(NP):
        own = p_occ.at[h, ylo, core, z]
        for q in order:
            remote(
                own, own, oz_s, oz_r.at[h, q], to(pair_at(ylo, lax.rem(z + q, nz), core), m)
            ).start()
        occ_on(h, 0)
    point(1)
    for h in range(NP):
        for q in order:
            occ_on(h, q)
        held = p_occ.at[h, ylo, core]
        remote(held, held, oc_s.at[h, 0], oc_r.at[h, 0], sibling).start()
    point(2)

    for copy in slab_copies:
        copy.wait()
    flip = (iota((chunk, chunk), 0) + iota((chunk, chunk), 1) == chunk - 1).astype(BF)
    nothing = jnp.zeros((chunk, chunk), BF)
    diag = jnp.concatenate(
        [
            jnp.sum(
                jnp.where(iota((16, pairs), 1) == target(j), low_diag[...].astype(F32), 0.0),
                axis=1, keepdims=True,
            )
            for j in range(per)
        ],
        axis=0,
    )
    row = p * 16 + lax.rem(iota((chunk, chunk), 0), 16)
    for k in range(mos):
        a = slab[:, :, half + k * chunk : half + (k + 1) * chunk].reshape(chunk, chunk).astype(F32)
        b = slab[:, :, half - (k + 1) * chunk : half - k * chunk].reshape(chunk, chunk)
        b = jnp.dot(b, flip, preferred_element_type=F32).astype(BF)
        col = k * chunk + iota((chunk, chunk), 1)
        a_low = jnp.where(col < row, a, jnp.where(col == row, a * 0.5, 0.0)).astype(BF)
        a_up = jnp.where(col > row, a, jnp.where(col == row, diag, 0.0)).astype(BF)
        left[k] = jnp.concatenate(
            [jnp.concatenate([a_low, b], axis=1), jnp.concatenate([nothing, a_up], axis=1)], axis=0
        )

    rest = pl.ds(0, (pairs - 1) * 16)

    def wait_raw(side):
        one = raw.at[side, pl.ds(0, 16)]
        pltpu.make_async_copy(one, one, raw_l.at[side]).wait()
        take(raw.at[side, rest], raw_r.at[side])

    def by_rows(a, b):
        return lax.dot_general(a, b, (((1,), (1,)), ((), ())), preferred_element_type=F32)

    def prepare_columns():
        same = (iota((chunk, chunk), 0) == iota((chunk, chunk), 1)).astype(BF)
        here = mine * chunk + iota((chunk, chunk), 0)
        wait_raw(1)
        for k in range(mos):
            there = k * chunk + iota((chunk, chunk), 1)
            a = by_rows(same, raw[1, k * chunk : (k + 1) * chunk])
            a_low = jnp.where(here < there, a, jnp.where(here == there, a * 0.5, 0.0))
            right[k, :chunk, :chunk] = a_low.astype(BF)
            right[k, :chunk, chunk:] = nothing
            right[k, chunk:, chunk:] = jnp.where(here > there, a, 0.0).astype(BF)

    prepare_columns()

    def occ_to_sibling(h):
        for k, step in enumerate((-1, 1, 2)):
            theirs = p_occ.at[h, lax.rem(ylo + step + YL, YL), core]
            take(theirs, oy_r.at[h, k])
            remote(theirs, theirs, oc_s.at[h, k + 1], oc_r.at[h, k + 1], sibling).start()
        for k in range(4):
            take(p_occ.at[0, 0, 0], oc_r.at[h, k])

    def blocks_of(k):
        firsts = [pairs // 2 + k * (chunk // 32) + b for b in range(chunk // 32)]
        for q in firsts + [pairs - 1 - q for q in firsts]:
            yield q // (nz * NC), q % NC, q // NC % nz

    def occ_rows(h, k):
        return jnp.concatenate([p_occ[(h, *at)] for at in blocks_of(k)], axis=0)

    def row_part(h):
        rows_sum = jnp.zeros((2 * chunk, ncol), F32)
        for k in range(mos):
            rows_sum += jnp.dot(left[k], occ_rows(h, k), preferred_element_type=F32)
        rows_sum = rows_sum.astype(BF)
        rp_send[h, :, 0:16] = rows_sum[:chunk].reshape(per, 16, ncol)
        rp_send[h, :, 16:32] = rows_sum[chunk:].reshape(per, 16, ncol)

        @pl.loop(0, per)
        def _(j):
            dst = rp.at[h, own_row]

            @pl.when(target(j) == p)
            def _():
                pltpu.make_async_copy(rp_send.at[h, j], dst, rp_r.at[h, own_row]).start()

            @pl.when(target(j) != p)
            def _():
                remote(
                    rp_send.at[h, j], dst, rp_s.at[h, j], rp_r.at[h, own_row], to(target(j), m)
                ).start()

    for h in range(NP):
        occ_to_sibling(h)
        row_part(h)
        point(3 + h)

    wait_raw(0)
    for k in range(mos):
        b = by_rows(flip, raw[0, k * chunk : (k + 1) * chunk]).astype(BF)
        right[k, chunk:, :chunk] = b
    column_sums = []
    for h in range(NP):
        column_sum = jnp.zeros((2 * chunk, ncol), F32)
        for k in range(mos):
            column_sum += jnp.dot(right[k], occ_rows(h, k), preferred_element_type=F32)
        column_sums.append(column_sum)

    other, base = (1 - yhi) * NX, yhi * NX

    def round_x(step):
        return to(p, base + lax.rem(x + step + NX, NX))

    def slot(h, first, step):
        return xo.at[first + lax.rem(x + step + NX, NX), h]

    def send_xo(h, which, ref, dev):
        remote(ref, ref, xo_s.at[h, which], xo_r.at[h, which], dev).start()

    def got_xo(h, which, ref):
        take(ref, xo_r.at[h, which])

    point(5)
    for h in range(NP):
        for j in range(per):
            take(rp.at[h, j], rp_r.at[h, j])
        row_sum = jnp.concatenate(
            [rp[h, :, 0:16].reshape(chunk, ncol), rp[h, :, 16:32].reshape(chunk, ncol)], axis=0
        )
        xo[m, h] = (column_sums[h] + row_sum.astype(F32)).astype(BF)
        send_xo(h, 0, xo.at[m, h], to(p, other + x))
        send_xo(h, 1, xo.at[m, h], round_x(1))
        send_xo(h, 2, xo.at[m, h], round_x(-1))
        send_xo(h, 3, xo.at[m, h], round_x(2))

    point(6)
    for h in range(NP):
        twin = xo.at[other + x, h]
        got_xo(h, 0, twin)
        send_xo(h, 4, twin, round_x(1))
        send_xo(h, 5, twin, round_x(-1))
        send_xo(h, 6, twin, round_x(2))
        if h == 0:
            point(7)
    point(8)

    take(p_vir.at[1 - core], vc_r)
    unit = (iota((256, 256), 0) == iota((256, 256), 1)).astype(BF)
    for k in range(mos):
        rows_k = jnp.concatenate([p_vir[c, z_, y_] for y_, c, z_ in blocks_of(k)], axis=0)
        left[k] = by_rows(unit, rows_k).astype(BF)

    def add(h, first, step, fresh=False):
        at = first + lax.rem(x + step + NX, NX)
        term = jnp.dot(left[block_of(p, at)], xo[at, h], preferred_element_type=F32)
        acc[h] = term if fresh else acc[h] + term

    for h in range(NP):
        add(h, base, 0, fresh=True)
        got_xo(h, 1, slot(h, base, -1))
        add(h, base, -1)
        add(h, other, 0)
    for h in range(NP):
        got_xo(h, 2, slot(h, base, 1))
        add(h, base, 1)
        got_xo(h, 5, slot(h, other, 1))
        add(h, other, 1)
    for h in range(NP):
        got_xo(h, 3, slot(h, base, 2))
        add(h, base, 2)
        got_xo(h, 4, slot(h, other, -1))
        add(h, other, -1)
    for h in range(NP):
        got_xo(h, 6, slot(h, other, 2))
        add(h, other, 2)
        out[0, :, h * ncol : (h + 1) * ncol] = acc[h, :nvir]

    take(part.at[pl.ds(0, mos - 1)], part_s)
    for h in range(NP):
        for k in range(3):
            take(p_occ.at[0, 0, 0], oy_s.at[h, k])
        for k in range(4):
            take(p_occ.at[0, 0, 0], oc_s.at[h, k])
    take(p_occ.at[:, 0, 0, pl.ds(0, nz - 1)], oz_s)
    for side in range(2):
        take(raw.at[side, rest], raw_s.at[side])
    take(p_vir.at[0, 0, pl.ds(0, YL - 1)], vy_s)
    for i in range(7):
        take(p_vir.at[0, 0], vz_s.at[i])
    take(p_vir.at[core], vc_s)

    @pl.loop(0, per)
    def _(j):
        @pl.when(target(j) != p)
        def _():
            for h in range(NP):
                take(rp_send.at[h, j], rp_s.at[h, j])

    for h in range(NP):
        for k in range(7):
            take(xo.at[0, 0], xo_s.at[h, k])


def shards(pairs, mos, packed, low_diag, occ_coef, vir_coef):
    per = pairs // mos
    chunk = 16 * per
    nz = pairs // (YL * NC)
    nocc = occ_coef.shape[1] * mos
    nvir = vir_coef.shape[1]
    dma = pltpu.SemaphoreType.DMA
    one = dma(())
    hbm = pl.BlockSpec(memory_space=pltpu.HBM)
    return pl.pallas_call(
        functools.partial(kernel, pairs, mos),
        out_shape=jax.ShapeDtypeStruct((1, nvir, nocc), F32),
        in_specs=[hbm] * 4,
        out_specs=pl.BlockSpec(memory_space=pltpu.VMEM),
        scratch_shapes=[
            pltpu.VMEM((2, 16 * pairs, chunk), BF),
            pltpu.VMEM((per, 16, packed.shape[2]), BF),
            pltpu.VMEM((mos, 16, 128), BF),
            pltpu.VMEM((NP, YL, NC, nz, 32, nocc // NP), BF),
            pltpu.VMEM((NC, nz, YL, 32, 256), BF),
            pltpu.VMEM((mos, 2 * chunk, 2 * chunk), BF),
            pltpu.VMEM((mos, 2 * chunk, 2 * chunk), BF),
            pltpu.VMEM((mos, NP, 2 * chunk, nocc // NP), BF),
            pltpu.VMEM((NP, per, 32, nocc // NP), BF),
            pltpu.VMEM((NP, per, 32, nocc // NP), BF),
            pltpu.VMEM((NP, 256, nocc // NP), F32),
            pltpu.VMEM(occ_coef.shape, BF),
            pltpu.VMEM(vir_coef.shape, BF),
            pltpu.VMEM((16, pairs), BF),
            dma((per + 3,)), dma((2,)), dma((2,)), dma((2,)), one, one,
            one, dma((NP, nz)), dma((NP, 3)), dma((NP, 3)), dma((NP, 4)), dma((NP, 4)),
            one, one, dma((7,)), dma((7,)), one, one,
            dma((NP, per)), dma((NP, per)), dma((NP, 7)), dma((NP, 7)),
        ],
        compiler_params=pltpu.CompilerParams(
            collective_id=0, has_side_effects=True, vmem_limit_bytes=62 * 1024 * 1024
        ),
    )(packed, low_diag.T, occ_coef, vir_coef).transpose(0, 2, 1)


def solution(mesh):
    sizes = dict(mesh.shape)
    placed = (P(None, "pair", None), P(None, "pair"), P("pair", "mo"), P("pair", "mo"))
    return jax.shard_map(
        functools.partial(shards, sizes["pair"], sizes["mo"]),
        mesh=mesh, in_specs=placed, out_specs=P("pair", None, "mo"), check_vma=False,
    )
```
